1024 devices in a mesh: dp: 16 (over y, core), expert: 64 (over z, x).
Axes of the slice: x: 8, y: 8, z: 8, core: 2. Of those that a mesh axis runs over, the one named last changes fastest.
Arguments:
- grad_out: bfloat16 [2048, 7168], P('expert', 'dp'), may hold values from -6 to 6
- probs: float32 [2048, 2], P('expert'), may hold values from 0.25 to 1
- expert_ids: int32 [2048, 2], P('expert'), may hold values from 0 to 3, all different within a row; in each aligned block of 32 rows (0 to 31, 32 to 63, ...) at most 32 rows name the same one
- x_saved: bfloat16 [4, 2048, 7168], P(None, None, 'dp'), may hold values from -6 to 6
- gate_act: bfloat16 [2048, 19456], P(None, 'expert'), may hold values from -6 to 6
- up_act: bfloat16 [2048, 19456], P(None, 'expert'), may hold values from -6 to 6
- w_up: bfloat16 [7168, 19456], P('dp', 'expert'), may hold values from -0.0625 to 0.0625
- w_down: bfloat16 [19456, 7168], P('expert', 'dp'), may hold values from -0.078125 to 0.078125
Outputs:
- grad_tokens: bfloat16 [2048, 7168], P('expert', 'dp')
- grad_w_up: bfloat16 [7168, 19456], P('dp', 'expert')
- grad_w_down: bfloat16 [19456, 7168], P('expert', 'dp')
The draws below stay inside these ranges and needn't reach their ends.
Inputs may be any that keep to these rules, and one draw needn't show every extreme that they name: `expert_ids`: the two experts of a token differ. Among the 32 tokens of one index of expert no expert is named more than 32 times, and in some such block one expert is named exactly 32 times.
All inputs are finite; a program needn't handle non-finite values.
Results may differ from the reference program's by a relative error of at most 0.0064.
Values may be sent and summed in bfloat16 or wider, within the bound.
A program may use at most 64 MiB of HBM per device.

```python
import math
import jax
import jax.numpy as jnp
import numpy as np
from jax import lax

D = 7168
FF = 4864
EXPERTS = 4
TOK_DEV = 32
CAP = 32
GROUP = 16
SLOTS = 2048
TOKENS = 2048
N_EXPERT = 64


def levels(own_key, extent, shards, least, high):
    def one(position, shards_of):
        steps = jax.random.uniform(jax.random.fold_in(jax.random.fold_in(own_key, 6), position), (shards_of,), jnp.float32, least / len(shards), high / len(shards))
        return jnp.repeat(jnp.exp(steps), extent[position] // shards_of).reshape((-1,) + (1,) * (len(extent) - position - 1))

    loudness = one(*shards[0])
    for cut in shards[1:]:
        loudness = loudness * one(*cut)
    return loudness


def routed_block(rng, own, number, rows, number_of, top, most, lean):
    ranking = jax.random.permutation(rng, number_of)
    crowded, usual = load_shares(number_of, rows * top, most, lean, True), load_shares(number_of, rows * top, most, lean, False)
    places = jnp.arange(number_of)

    def named(lengths, turn):
        used = int((lengths > 0).sum())
        fixed = max(1, used // 4)
        moved = fixed + (places - fixed + turn * (used - fixed)) % max(1, number_of - fixed)
        return jnp.zeros((number_of,), jnp.int32).at[ranking[jnp.where(places < fixed, places, moved)]].set(jnp.asarray(lengths, jnp.int32))

    lengths = jnp.where(number % 4 == 0, named(crowded, number // 4), named(usual, number - number // 4 - 1))
    mixed = jax.random.permutation(jax.random.fold_in(own, 3), number_of)
    source_of, taker = mixed[0:number_of // 2 * 2:2], mixed[1:number_of // 2 * 2:2]
    room = jnp.minimum(lengths[source_of] - 1, most - lengths[taker]) // 2
    room = jnp.where((source_of == ranking[0]) | (taker == ranking[0]) | (lengths[taker] == 0), 0, jnp.maximum(room, 0))
    moved = jax.random.randint(jax.random.fold_in(own, 4), (number_of // 2,), 0, 1 << 20) % (room + 1)
    lengths = lengths.at[source_of].add(-moved).at[taker].add(moved)
    members = jnp.searchsorted(jnp.cumsum(lengths), jnp.arange(rows * top), side="right").astype(jnp.int32)
    listing = members.reshape(top, rows).T
    listing = listing[jax.random.permutation(jax.random.fold_in(own, 1), rows)]
    turn = jax.random.randint(jax.random.fold_in(own, 2), (rows, 1), 0, top)
    return jnp.take_along_axis(listing, (jnp.arange(top)[None, :] + turn) % top, axis=1)


def load_shares(amount, total, limit, slope, full):
    weights = [(1 << 20) // math.isqrt(rank ** slope) + 1 for rank in range(1, amount + 1)]
    largest = limit if full else min(limit, max(-(-total // amount), total * weights[0] // sum(weights)))
    least = 1 if total - largest >= amount - 1 else 0
    counts, spare = [largest] + [least] * (amount - 1), total - largest - least * (amount - 1)
    while spare > 0:
        movable = [i for i in range(1, amount) if counts[i] < largest] or [i for i in range(1, amount) if counts[i] < limit]
        mass, remaining = sum([weights[i] for i in movable]), spare
        for i in movable:
            extra = min(limit - counts[i], max(1, remaining * weights[i] // mass), spare)
            counts[i] = counts[i] + extra
            spare = spare - extra
    return np.array(counts)


def gaussian(stream_key, extent, spread, reach, shards=(), held_as=jnp.bfloat16):
    drawn = spread * jax.random.normal(stream_key, extent, jnp.float32)
    if shards:
        drawn = drawn * levels(stream_key, extent, shards, -0.22, 0.18)
    return jnp.clip(drawn, -reach, reach).astype(held_as)


def setup_inputs(seed: int = 0) -> dict:
    splits = jax.random.split(jax.random.key(seed), 9)
    grad_out = gaussian(splits[0], (TOKENS, D), 1.0, 6.0, ((0, 64), (1, 16)))
    probs = jnp.clip(0.25 + 0.75 * jax.random.uniform(splits[1], (TOKENS, 2), jnp.float32) ** levels(splits[1], (TOKENS, 2), ((0, 64),), -0.2, 0.2), 0.25, 1.0)
    expert_ids_keys = jax.random.split(jax.random.fold_in(splits[2], 1), TOKENS // TOK_DEV)
    expert_ids_turns = jax.random.permutation(jax.random.fold_in(splits[2], 3), TOKENS // TOK_DEV)
    expert_ids = jax.vmap(lambda own, number: routed_block(jax.random.fold_in(splits[2], 2), own, number, TOK_DEV, EXPERTS, 2, CAP, 2))(expert_ids_keys, expert_ids_turns).reshape((TOKENS, 2))
    x_saved = gaussian(splits[3], (EXPERTS, SLOTS, D), 1.0, 6.0, ((2, 16),))
    gate_act = gaussian(splits[4], (SLOTS, EXPERTS * FF), 1.0, 6.0, ((1, 64),))
    up_act = gaussian(splits[5], (SLOTS, EXPERTS * FF), 1.0, 6.0, ((1, 64),))
    w_up = gaussian(splits[6], (D, EXPERTS * FF), D ** -0.5, 0.0625, ((0, 16), (1, 64)))
    w_down = gaussian(splits[7], (EXPERTS * FF, D), FF ** -0.5, 0.078125, ((0, 64), (1, 16)))
    return dict(grad_out=grad_out, probs=probs, expert_ids=expert_ids, x_saved=x_saved, gate_act=gate_act, up_act=up_act, w_up=w_up, w_down=w_down)


def slot_ranks(flat_ids):
    onehot = (flat_ids[:, :, None] == jnp.arange(EXPERTS, dtype=jnp.int32)[None, None, :]).astype(jnp.int32)
    before = jnp.cumsum(onehot, axis=1) - onehot
    return jnp.sum(before * onehot, axis=2).astype(jnp.int32)


def reference(grad_out, probs, expert_ids, x_saved, gate_act, up_act, w_up, w_down):
    flat_ids = expert_ids.reshape(N_EXPERT, 2 * TOK_DEV).astype(jnp.int32)
    slot_rank = slot_ranks(flat_ids)
    source = jnp.broadcast_to(jnp.arange(N_EXPERT, dtype=jnp.int32)[:, None], flat_ids.shape)
    scaled = (probs[:, :, None] * grad_out[:, None, :].astype(jnp.float32)).astype(jnp.bfloat16)
    scaled = scaled.reshape(N_EXPERT, 2 * TOK_DEV, D)
    routed = jnp.zeros((EXPERTS, CAP, N_EXPERT, D), jnp.bfloat16).at[flat_ids, slot_rank, source].set(scaled)
    routed = routed.reshape(EXPERTS, SLOTS, D)
    block_width = FF // GROUP
    up_grads = []
    down_grads = []
    slot_list = []
    for expert in range(EXPERTS):
        low_col = expert * FF
        gate_vals = gate_act[:, low_col:low_col + FF].astype(jnp.float32)
        up_vals = up_act[:, low_col:low_col + FF].astype(jnp.float32)
        down_rows = w_down[low_col:low_col + FF]
        up_cols = w_up[:, low_col:low_col + FF]
        hidden_back = jnp.dot(routed[expert], down_rows.T, preferred_element_type=jnp.float32)
        unit_grad = (hidden_back * gate_vals).astype(jnp.bfloat16)
        hidden = (gate_vals * up_vals).astype(jnp.bfloat16)
        down_grads.append(jnp.dot(hidden.T, routed[expert], preferred_element_type=jnp.float32).astype(jnp.bfloat16))
        up_grads.append(jnp.dot(x_saved[expert].T, unit_grad, preferred_element_type=jnp.float32).astype(jnp.bfloat16))
        slot_sum = jnp.zeros((SLOTS, D), jnp.float32)
        for block_index in range(GROUP):
            first_col = block_index * block_width
            block_term = jnp.dot(unit_grad[:, first_col:first_col + block_width],
                                 up_cols[:, first_col:first_col + block_width].T,
                                 preferred_element_type=jnp.float32)
            slot_sum = slot_sum + lax.optimization_barrier(block_term.astype(jnp.bfloat16)).astype(jnp.float32)
        slot_list.append(slot_sum)
    slot_grads = jnp.stack(slot_list).reshape(EXPERTS, CAP, N_EXPERT, D)
    picked = slot_grads[flat_ids, slot_rank, source]
    grad_tokens = jnp.sum(picked.reshape(TOKENS, 2, D), axis=1).astype(jnp.bfloat16)
    return grad_tokens, jnp.concatenate(up_grads, axis=1), jnp.concatenate(down_grads, axis=0)
```

```python
import functools

import jax
import jax.numpy as jnp
from jax import lax
from jax.experimental import pallas as pl
from jax.experimental.pallas import tpu as pltpu
from jax.sharding import PartitionSpec as P

F32, BF16 = jnp.float32, jnp.bfloat16
MESH = pl.DeviceIdType.MESH
N = 8
TOK = 32
CAP = 32
EXPERTS = 4
GROUPS = 4
ROWS = 16 * TOK
SPLIT = ((0, 160), (160, 144))


def hops(right, piece):
    return N // 2 if right == (piece == 0) else N // 2 - 1


def add(a, b):
    return a.astype(F32) + b.astype(F32)


def kernel(
    g_ref, probs_ref, ids_ref, x_hbm, gate_hbm, up_hbm, wup_hbm, wdown_hbm,
    tok_out, gup_out, gdown_out,
    shard, gath, place, routed, wdown, wup, gate, up, xt, part, pair, unit, terms, tok,
    yrecv, drecv, reduced, final,
    ld_sem, s1, r1, s2, r2, cs, cr, ys, yr, us, ur, fs, fr, ds, dr, es, er,
):
    pos, dpos = lax.axis_index("expert"), lax.axis_index("dp")
    z, x = pos // N, pos % N
    y, core = dpos // 2, dpos % 2
    expert = pos // (N * N // EXPERTS)

    def on_x(d):
        return {"expert": z * N + (x + d + N) % N}

    def on_z(d):
        return {"expert": ((z + d + N) % N) * N + x}

    def on_y(d):
        return {"dp": ((y + d + N) % N) * 2 + core}

    other = {"dp": y * 2 + (1 - core)}

    def remote(src, dst, ssem, rsem, dev):
        return pltpu.make_async_remote_copy(
            src_ref=src, dst_ref=dst, send_sem=ssem, recv_sem=rsem, device_id=dev, device_id_type=MESH
        )

    loads = [
        pltpu.make_async_copy(wdown_hbm, wdown, ld_sem.at[0]),
        pltpu.make_async_copy(gate_hbm, gate, ld_sem.at[1]),
        pltpu.make_async_copy(up_hbm, up, ld_sem.at[2]),
        pltpu.make_async_copy(wup_hbm, wup, ld_sem.at[3]),
        pltpu.make_async_copy(x_hbm.at[expert], xt, ld_sem.at[4]),
    ]
    for load in loads:
        load.start()

    barrier = pltpu.get_barrier_semaphore()
    partners = [on_x(d) for d in range(1, N)] + [on_z(d) for d in range(1, N)] + [on_y(1), on_y(-1), other]
    for dev in partners:
        pl.semaphore_signal(barrier, inc=1, device_id=dev, device_id_type=MESH)

    lane32 = lax.broadcasted_iota(jnp.int32, (TOK, TOK), 1)
    row32 = lax.broadcasted_iota(jnp.int32, (TOK, TOK), 0)
    lane128 = lax.broadcasted_iota(jnp.int32, (TOK, 128), 1)
    tail = g_ref[:, 384:512].astype(F32)
    for e in range(EXPERTS):
        named = ids_ref[...] == e
        prob_row = jnp.sum(jnp.where(named, probs_ref[...], 0.0), axis=0, keepdims=True)
        used_row = jnp.sum(jnp.where(named, 1.0, 0.0), axis=0, keepdims=True)
        prob = jnp.sum(jnp.where(lane32 == row32, prob_row, 0.0), axis=1, keepdims=True)
        used = jnp.sum(jnp.where(lane32 == row32, used_row, 0.0), axis=1, keepdims=True)
        before = jnp.sum(jnp.where(lane32 < row32, used_row, 0.0), axis=1, keepdims=True)
        high = prob.astype(BF16).astype(F32)
        middle = (prob - high).astype(BF16).astype(F32)
        rank = used * (before + 1.0) - 1.0
        for i, column in enumerate((high, middle, prob - high - middle, rank)):
            tail = jnp.where(lane128 == 64 + 4 * e + i, column, tail)
    shard[:, 0:384] = g_ref[:, 0:384]
    shard[:, 384:512] = tail.astype(BF16)
    gath[z, x, 0] = shard[0:16, :]
    gath[z, x, 1] = shard[16:32, :]

    pl.semaphore_wait(barrier, len(partners))

    first = []
    for d in range(1, N):
        for h, to in ((0, on_x), (1, on_z)):
            first.append(remote(gath.at[z, x, h], gath.at[z, x, h], s1.at[h, d - 1], r1.at[h, d - 1], to(d)))
            first[-1].start()
    for copy in first:
        copy.wait_recv()
    sent = list(first)

    def block(ref, h, index, piece):
        if h == 0:
            return ref.at[index, pl.ds(4 * piece, 4), 0]
        return ref.at[pl.ds(4 * piece, 4), index, 1]

    along = (on_z, on_x)
    here = (z, x)
    inflight = {}
    for k in range(N // 2):
        for c in range(2):
            for h in range(2):
                for r in range(2):
                    sign = 1 if r else -1
                    if k >= 1 and k - 1 < hops(r, c):
                        inflight[k - 1, c, h, r].wait_recv()
                    if k < hops(r, c):
                        view = block(gath, h, (here[h] - sign * k + N) % N, c)
                        copy = remote(view, view, s2.at[k, c, h, r], r2.at[k, c, h, r], along[h](sign))
                        copy.start()
                        inflight[k, c, h, r] = copy
                        sent.append(copy)
    for c in range(2):
        for h in range(2):
            for r in range(2):
                if hops(r, c) == N // 2:
                    inflight[N // 2 - 1, c, h, r].wait_recv()

    lane_id = lax.broadcasted_iota(jnp.int32, (ROWS, ROWS), 1)
    source = lax.broadcasted_iota(jnp.int32, (ROWS, 1), 0) // TOK
    tail_lane = lax.broadcasted_iota(jnp.int32, (ROWS, 128), 1) - 64 - 4 * expert

    def to_slots(g, carry):
        rows = gath[pl.ds(2 * g, 2)].reshape(ROWS, 512)
        extra = rows[:, 384:512].astype(F32)
        weight = jnp.sum(jnp.where((tail_lane >= 0) & (tail_lane < 3), extra, 0.0), axis=1, keepdims=True)
        rank = jnp.sum(jnp.where(tail_lane == 3, extra, 0.0), axis=1, keepdims=True)
        key = rank.astype(jnp.int32) * 16 + source
        onehot = jnp.where(key == lane_id, 1.0, 0.0).astype(BF16)
        place[g] = onehot
        scaled = (rows.astype(F32) * weight).astype(BF16)
        moved = lax.dot_general(onehot, scaled, (((0,), (0,)), ((), ())), preferred_element_type=F32)
        start = pl.multiple_of(16 * g, 16)
        routed[:, pl.ds(start, 16), :] = moved[:, 0:448].astype(BF16).reshape(CAP, 16, 448)
        return carry

    lax.fori_loop(0, GROUPS, to_slots, 0)

    loads[0].wait()

    def partial(b, carry):
        rows = routed[pl.ds(2 * b, 2)].reshape(128, 448)
        part[b] = lax.dot_general(
            wdown[...], rows, (((1,), (1,)), ((), ())), preferred_element_type=F32
        ).astype(BF16)
        return carry

    cross = []
    for i in range(N):
        lax.fori_loop((1 - core) * N + i, (1 - core) * N + i + 1, partial, 0)
        copy = remote(part.at[(1 - core) * N + i], pair.at[i], cs.at[i], cr.at[i], other)
        copy.start()
        cross.append(copy)
        sent.append(copy)
    lax.fori_loop(core * N, core * N + N, partial, 0)
    for i in range(N):
        cross[i].wait_recv()
        pair[i] = add(pair[i], part[core * N + i]).astype(BF16)

    inflight = {}
    for k in range(N // 2):
        for c, (low, size) in enumerate(SPLIT):
            for r in range(2):
                sign, far = (1 if r else -1), hops(r, c)
                target = (y + sign * (far - k) + N) % N
                view = pair.at[target, pl.ds(low, size)]
                if k >= 1 and k < far:
                    inflight[k - 1, c, r].wait_recv()
                    view[...] = add(view[...], yrecv[k - 1, c, r, 0:size]).astype(BF16)
                if k < far:
                    copy = remote(
                        view, yrecv.at[k, c, r, pl.ds(0, size)], ys.at[k, c, r], yr.at[k, c, r], on_y(sign)
                    )
                    copy.start()
                    inflight[k, c, r] = copy
                    sent.append(copy)
    for load in loads[1:]:
        load.wait()
    mine = core * N + y
    lanes = pl.ds(pl.multiple_of(mine * 128, 128), 128)
    for c, (low, size) in enumerate(SPLIT):
        total = pair[y, low:low + size].astype(F32)
        for r in range(2):
            inflight[hops(r, c) - 1, c, r].wait_recv()
            total = total + yrecv[hops(r, c) - 1, c, r, 0:size].astype(F32)
        unit[mine, low:low + size] = (total * gate[low:low + size, lanes].astype(F32)).astype(BF16)

    inflight = {}
    across = []

    def cross_piece(index, c, slot):
        view = unit.at[core * N + index, pl.ds(SPLIT[c][0], SPLIT[c][1])]
        copy = remote(view, view, fs.at[slot, c], fr.at[slot, c], other)
        copy.start()
        across.append(copy)
        sent.append(copy)

    for k in range(N // 2 + 1):
        for c, (low, size) in enumerate(SPLIT):
            for r in range(2):
                sign, far = (1 if r else -1), hops(r, c)
                index = (y - sign * k + N) % N
                if k >= 1 and k <= far:
                    inflight[k - 1, c, r].wait_recv()
                if k < far:
                    view = unit.at[core * N + index, pl.ds(low, size)]
                    copy = remote(view, view, us.at[k, c, r], ur.at[k, c, r], on_y(sign))
                    copy.start()
                    inflight[k, c, r] = copy
                    sent.append(copy)
                if (k == 0 and r == 0) or (1 <= k <= far):
                    cross_piece(index, c, (sign * k + N) % N)

    def down_block(b, carry):
        span = pl.ds(pl.multiple_of(b * 512, 512), 512)
        hidden = (gate[:, span].astype(F32) * up[:, span].astype(F32)).astype(BF16)
        rows = routed[pl.ds(8 * b, 8)].reshape(512, 448)
        return carry + jnp.dot(hidden, rows, preferred_element_type=F32)

    gdown_out[...] = lax.fori_loop(0, 4, down_block, jnp.zeros((304, 448), F32)).astype(BF16)
    for copy in across:
        copy.wait_recv()

    def slot_block(b, carry):
        rows = lax.dot_general(unit[b], wup[...], (((0,), (0,)), ((), ())), preferred_element_type=F32)
        terms[pl.ds(2 * b, 2)] = rows.astype(BF16).reshape(2, 64, 448)
        return carry

    lax.fori_loop(0, 2 * N, slot_block, 0)

    def to_tokens(g, carry):
        start = pl.multiple_of(16 * g, 16)
        rows = terms[:, pl.ds(start, 16), :].reshape(ROWS, 448)
        back = jnp.dot(place[g], rows, preferred_element_type=F32).astype(BF16)
        tok[pl.ds(2 * g, 2)] = back.reshape(2, N, 2, 16, 448)
        return carry

    lax.fori_loop(0, GROUPS, to_tokens, 0)

    inflight = {}
    for k in range(N // 2):
        for c in range(2):
            for h in range(2):
                for r in range(2):
                    sign, far = (1 if r else -1), hops(r, c)
                    view = block(tok, h, (here[h] + sign * (far - k) + N) % N, c)
                    if k >= 1 and k < far:
                        inflight[k - 1, c, h, r].wait_recv()
                        view[...] = add(view[...], drecv[k - 1, c, h, r]).astype(BF16)
                    if k < far:
                        copy = remote(view, drecv.at[k, c, h, r], ds.at[k, c, h, r], dr.at[k, c, h, r], along[h](sign))
                        copy.start()
                        inflight[k, c, h, r] = copy
                        sent.append(copy)

    def up_block(b, carry):
        span = pl.ds(pl.multiple_of(b * 128, 128), 128)
        return carry + lax.dot_general(unit[b], xt[:, span], (((1,), (1,)), ((), ())), preferred_element_type=F32)

    gup_out[...] = lax.fori_loop(0, 2 * N, up_block, jnp.zeros((304, 448), F32)).astype(BF16)

    for h in range(2):
        for c in range(2):
            total = block(tok, h, here[h], c)[...].astype(F32)
            for r in range(2):
                inflight[hops(r, c) - 1, c, h, r].wait_recv()
                total = total + drecv[hops(r, c) - 1, c, h, r].astype(F32)
            reduced[h, 4 * c:4 * c + 4] = total.astype(BF16)
    last = []
    for d in range(1, N):
        for h, to in ((0, on_x), (1, on_z)):
            away = (here[1 - h] + d) % N
            copy = remote(reduced.at[h, away], final.at[h, d - 1], es.at[h, d - 1], er.at[h, d - 1], to(d))
            copy.start()
            last.append(copy)
            sent.append(copy)
    for copy in last:
        copy.wait_recv()
    for h in range(2):
        total = reduced[h, here[1 - h]].astype(F32)
        for d in range(1, N):
            total = total + final[h, d - 1].astype(F32)
        tok_out[16 * h:16 * h + 16, :] = total.astype(BF16)
    for copy in sent:
        copy.wait_send()


def body(grad_out, probs, expert_ids, x_saved, gate_act, up_act, w_up, w_down):
    vmem, hbm = pl.BlockSpec(memory_space=pltpu.VMEM), pl.BlockSpec(memory_space=pl.ANY)
    dma = pltpu.SemaphoreType.DMA
    units, width, slots = 304, 448, 2048
    outs = pl.pallas_call(
        kernel,
        out_shape=(
            jax.ShapeDtypeStruct((TOK, width), BF16),
            jax.ShapeDtypeStruct((units, width), BF16),
            jax.ShapeDtypeStruct((units, width), BF16),
        ),
        in_specs=[vmem, vmem, vmem, hbm, hbm, hbm, hbm, hbm],
        out_specs=(vmem, vmem, vmem),
        scratch_shapes=[
            pltpu.VMEM((TOK, 512), BF16),
            pltpu.VMEM((N, N, 2, 16, 512), BF16),
            pltpu.VMEM((GROUPS, ROWS, ROWS), BF16),
            pltpu.VMEM((CAP, N * N, width), BF16),
            pltpu.VMEM((units, width), BF16),
            pltpu.VMEM((units, width), BF16),
            pltpu.VMEM((units, slots), BF16),
            pltpu.VMEM((units, slots), BF16),
            pltpu.VMEM((width, slots), BF16),
            pltpu.VMEM((2 * N, units, 128), BF16),
            pltpu.VMEM((N, units, 128), BF16),
            pltpu.VMEM((2 * N, units, 128), BF16),
            pltpu.VMEM((CAP, N * N, width), BF16),
            pltpu.VMEM((N, N, 2, 16, width), BF16),
            pltpu.VMEM((4, 2, 2, 160, 128), BF16),
            pltpu.VMEM((4, 2, 2, 2, 4, 16, width), BF16),
            pltpu.VMEM((2, N, 16, width), BF16),
            pltpu.VMEM((2, N - 1, 16, width), BF16),
            dma((5,)),
            dma((2, N - 1)), dma((2, N - 1)),
            dma((4, 2, 2, 2)), dma((4, 2, 2, 2)),
            dma((N,)), dma((N,)),
            dma((4, 2, 2)), dma((4, 2, 2)),
            dma((4, 2, 2)), dma((4, 2, 2)),
            dma((N, 2)), dma((N, 2)),
            dma((4, 2, 2, 2)), dma((4, 2, 2, 2)),
            dma((2, N - 1)), dma((2, N - 1)),
        ],
        compiler_params=pltpu.CompilerParams(
            collective_id=0, has_side_effects=True, vmem_limit_bytes=48 * 1024 * 1024
        ),
        cost_estimate=pl.CostEstimate(flops=4_000_000_000, bytes_accessed=8_000_000, transcendentals=0),
    )(
        jnp.pad(grad_out, ((0, 0), (0, 64))),
        probs.T,
        expert_ids.T,
        jnp.swapaxes(x_saved, 1, 2),
        gate_act.T,
        up_act.T,
        w_up.T,
        w_down,
    )
    return outs[0], outs[1].T, outs[2]


def solution(mesh):
    return jax.shard_map(
        body,
        mesh=mesh,
        in_specs=(
            P("expert", "dp"),
            P("expert", None),
            P("expert", None),
            P(None, None, "dp"),
            P(None, "expert"),
            P(None, "expert"),
            P("dp", "expert"),
            P("expert", "dp"),
        ),
        out_specs=(P("expert", "dp"), P("dp", "expert"), P("expert", "dp")),
        check_vma=False,
    )
```

```python
import functools

import jax
import jax.numpy as jnp
from jax import lax
from jax.experimental import pallas as pl
from jax.experimental.pallas import tpu as pltpu
from jax.sharding import PartitionSpec as P

F32, BF16 = jnp.float32, jnp.bfloat16
MESH = pl.DeviceIdType.MESH
N = 8
TOK = 32
CAP = 32
EXPERTS = 4
GROUPS = 4
ROWS = 16 * TOK
SPLIT = ((0, 80), (80, 80), (160, 80), (240, 64))
HALVES = ((0, 160), (160, 144))
PIECES = 4


def hops(right, piece):
    return N // 2 if right == (piece < 2) else N // 2 - 1


def add(a, b):
    return a.astype(F32) + b.astype(F32)


def kernel(
    g_hbm, probs_hbm, ids_hbm, x_hbm, gate_hbm, up_hbm, wup_hbm, wdown_hbm,
    tok_out, gup_out, gdown_out,
    g_ref, probs_ref, ids_ref, shard, gath, place, routed, routed2, wdown, wdown2, wup, gate, up, xt, pair, unit, terms,
    tok, yrecv, drecv, reduced, final, down_sum,
    ld_sem, s1, r1, s2, r2, ws, wr, cs, cr, ys, yr, us, ur, fs, fr, ds, dr, es, er,
):
    pos, dpos = lax.axis_index("expert"), lax.axis_index("dp")
    z, x = pos // N, pos % N
    y, core = dpos // 2, dpos % 2
    expert = pos // (N * N // EXPERTS)

    def on_x(d):
        return {"expert": z * N + (x + d + N) % N}

    def on_z(d):
        return {"expert": ((z + d + N) % N) * N + x}

    def on_y(d):
        return {"dp": ((y + d + N) % N) * 2 + core}

    other = {"dp": y * 2 + (1 - core)}
    along = (on_z, on_x)
    here = (z, x)
    sent = []

    def remote(src, dst, ssem, rsem, dev):
        copy = pltpu.make_async_remote_copy(
            src_ref=src, dst_ref=dst, send_sem=ssem, recv_sem=rsem, device_id=dev, device_id_type=MESH
        )
        copy.start()
        sent.append(copy)
        return copy

    loads = [
        pltpu.make_async_copy(g_hbm, g_ref, ld_sem.at[0]),
        pltpu.make_async_copy(probs_hbm, probs_ref, ld_sem.at[1]),
        pltpu.make_async_copy(ids_hbm, ids_ref, ld_sem.at[2]),
        pltpu.make_async_copy(wdown_hbm, wdown, ld_sem.at[3]),
        pltpu.make_async_copy(gate_hbm, gate, ld_sem.at[4]),
        pltpu.make_async_copy(up_hbm, up, ld_sem.at[5]),
        pltpu.make_async_copy(wup_hbm, wup, ld_sem.at[6]),
        pltpu.make_async_copy(x_hbm.at[expert], xt, ld_sem.at[7]),
    ]
    for load in loads:
        load.start()

    barrier = pltpu.get_barrier_semaphore()
    partners = [on_x(d) for d in range(1, N)] + [on_z(d) for d in range(1, N)] + [on_y(1), on_y(-1), other]
    for dev in partners:
        pl.semaphore_signal(barrier, inc=1, device_id=dev, device_id_type=MESH)

    for load in loads[0:3]:
        load.wait()
    lane32 = lax.broadcasted_iota(jnp.int32, (TOK, TOK), 1)
    row32 = lax.broadcasted_iota(jnp.int32, (TOK, TOK), 0)
    lane128 = lax.broadcasted_iota(jnp.int32, (TOK, 128), 1)
    shard[:, 384:512] = jnp.zeros((TOK, 128), BF16)
    shard[:, 0:448] = g_ref[...]
    tail = shard[:, 384:512].astype(F32)
    for e in range(EXPERTS):
        named = ids_ref[...] == e
        prob_row = jnp.sum(jnp.where(named, probs_ref[...], 0.0), axis=0, keepdims=True)
        used_row = jnp.sum(jnp.where(named, 1.0, 0.0), axis=0, keepdims=True)
        prob = jnp.sum(jnp.where(lane32 == row32, prob_row, 0.0), axis=1, keepdims=True)
        used = jnp.sum(jnp.where(lane32 == row32, used_row, 0.0), axis=1, keepdims=True)
        before = jnp.sum(jnp.where(lane32 < row32, used_row, 0.0), axis=1, keepdims=True)
        high = prob.astype(BF16).astype(F32)
        middle = (prob - high).astype(BF16).astype(F32)
        rank = used * (before + 1.0) - 1.0
        for i, column in enumerate((high, middle, prob - high - middle, rank)):
            tail = jnp.where(lane128 == 64 + 4 * e + i, column, tail)
    shard[:, 384:512] = tail.astype(BF16)
    for h in range(2):
        gath[h, here[h], 0] = shard[16 * h:16 * h + 16, :]
    loads[3].wait()

    pl.semaphore_wait(barrier, len(partners))

    first = {}
    for d in (1, 7, 2, 6, 3, 5, 4):
        for h in range(2):
            first[h, N - d] = remote(
                gath.at[h, here[h], 0], gath.at[h, here[h], N - d], s1.at[h, d - 1], r1.at[h, N - d - 1], along[1 - h](d)
            )
    down_swap = remote(wdown, wdown2, ws.at[0], wr.at[0], other)

    def piece(ref, h, index, c):
        return ref.at[h, index, pl.ds(2 * c, 2)]

    inflight = {}
    for k in range(N // 2 + 1):
        for c in (0, 3, 1, 2):
            for h in range(2):
                if k == 0:
                    for j in (2 * c, 2 * c + 1):
                        if j > 0:
                            first[h, j].wait_recv()
                for r in range(2):
                    sign, far = (1 if r else -1), hops(r, c)
                    if 1 <= k <= far:
                        inflight[k - 1, c, h, r].wait_recv()
                    if k < far:
                        view = piece(gath, h, (here[h] - sign * k + N) % N, c)
                        inflight[k, c, h, r] = remote(
                            view, view, s2.at[k, c, h, r], r2.at[k, c, h, r], along[h](sign)
                        )

    lane_id = lax.broadcasted_iota(jnp.int32, (ROWS, ROWS), 1)
    row_id = lax.broadcasted_iota(jnp.int32, (ROWS, 1), 0)
    tile = (row_id % 256) // 16
    source = jnp.where(
        row_id < 256, (tile // 8) * 8 + (tile % 8 + x) % 8, (tile // 8) * 8 + tile % 8
    )
    tail_lane = lax.broadcasted_iota(jnp.int32, (ROWS, 128), 1) - 64 - 4 * expert

    def swap(g):
        span = pl.ds(pl.multiple_of(16 * g, 16), 16)
        return pltpu.make_async_remote_copy(
            src_ref=routed.at[pl.ds((1 - core) * 16, 16), span], dst_ref=routed2.at[:, span],
            send_sem=cs.at[g], recv_sem=cr.at[g], device_id=other, device_id_type=MESH,
        )

    def to_slots(g, carry):
        one = gath[0, pl.ds(2 * g, 2)].reshape(256, 512)
        two = gath[1, :, (2 * g - z + N) % N].reshape(128, 512)
        three = gath[1, :, (2 * g + 1 - z + N) % N].reshape(128, 512)
        rows = jnp.concatenate([one, two, three], axis=0)
        extra = rows[:, 384:512].astype(F32)
        weight = jnp.sum(jnp.where((tail_lane >= 0) & (tail_lane < 3), extra, 0.0), axis=1, keepdims=True)
        rank = jnp.sum(jnp.where(tail_lane == 3, extra, 0.0), axis=1, keepdims=True)
        key = rank.astype(jnp.int32) * 16 + source
        onehot = jnp.where(key == lane_id, 1.0, 0.0).astype(BF16)
        place[g] = onehot
        scaled = (rows.astype(F32) * weight).astype(BF16)
        moved = lax.dot_general(onehot, scaled, (((0,), (0,)), ((), ())), preferred_element_type=F32)
        start = pl.multiple_of(16 * g, 16)
        routed[:, pl.ds(start, 16), :] = moved[:, 0:448].astype(BF16).reshape(CAP, 16, 448)
        swap(g).start()
        return carry

    lax.fori_loop(0, GROUPS, to_slots, 0)

    down_swap.wait_recv()
    for g in range(GROUPS):
        swap(g).wait_recv()

    def partial(i):
        mine = routed[pl.ds(core * 16 + 2 * i, 2)].reshape(128, 448)
        theirs = routed2[pl.ds(2 * i, 2)].reshape(128, 448)
        dims = (((1,), (1,)), ((), ()))
        pair[i] = (
            lax.dot_general(wdown[...], mine, dims, preferred_element_type=F32)
            + lax.dot_general(wdown2[...], theirs, dims, preferred_element_type=F32)
        ).astype(BF16)

    def down_block(b):
        span = pl.ds(512 * b, 512)
        hidden = (gate[:, span].astype(F32) * up[:, span].astype(F32)).astype(BF16)
        rows = routed[8 * b:8 * b + 8].reshape(512, 448)
        product = jnp.dot(hidden, rows, preferred_element_type=F32)
        if b == 0:
            down_sum[...] = product
        elif b < 3:
            down_sum[...] += product
        else:
            gdown_out[...] = (down_sum[...] + product).astype(BF16)

    inflight = {}
    for far in (4, 3):
        for offset in ((4,) if far == 4 else (3, -3)):
            partial((y + offset + N) % N)
        for c, (low, size) in enumerate(SPLIT):
            for r in range(2):
                if hops(r, c) == far:
                    view = pair.at[(y + (far if r else -far) + N) % N, pl.ds(low, size)]
                    inflight[0, c, r] = remote(
                        view, yrecv.at[0, c, r, pl.ds(0, size)], ys.at[0, c, r], yr.at[0, c, r], on_y(1 if r else -1)
                    )
    for offset in (2, -2, 1, -1, 0):
        partial((y + offset + N) % N)
    for k in range(1, N // 2):
        for c, (low, size) in enumerate(SPLIT):
            for r in range(2):
                sign, far = (1 if r else -1), hops(r, c)
                if k < far:
                    view = pair.at[(y + sign * (far - k) + N) % N, pl.ds(low, size)]
                    inflight[k - 1, c, r].wait_recv()
                    view[...] = add(view[...], yrecv[k - 1, c, r, 0:size]).astype(BF16)
                    inflight[k, c, r] = remote(
                        view, yrecv.at[k, c, r, pl.ds(0, size)], ys.at[k, c, r], yr.at[k, c, r], on_y(sign)
                    )
        if k == 1:
            for load in loads[4:6]:
                load.wait()
        down_block(k - 1)
    for load in loads[6:]:
        load.wait()

    mine = core * N + y
    lanes = pl.ds(pl.multiple_of(mine * 128, 128), 128)
    gathering = {}
    for c, (low, size) in enumerate(SPLIT):
        total = pair[y, low:low + size].astype(F32)
        for r in range(2):
            inflight[hops(r, c) - 1, c, r].wait_recv()
            total = total + yrecv[hops(r, c) - 1, c, r, 0:size].astype(F32)
        unit[mine, low:low + size] = (total * gate[low:low + size, lanes].astype(F32)).astype(BF16)
        view = unit.at[mine, pl.ds(low, size)]
        for r in range(2):
            gathering[0, c, r] = remote(view, view, us.at[0, c, r], ur.at[0, c, r], on_y(1 if r else -1))
    across = {}

    def cross_half(k, h, r, index):
        view = unit.at[core * N + index, pl.ds(HALVES[h][0], HALVES[h][1])]
        across[k, h, r] = remote(view, view, fs.at[k, h, r], fr.at[k, h, r], other)

    def slot_block(b):
        rows = lax.dot_general(unit[b], wup[...], (((0,), (0,)), ((), ())), preferred_element_type=F32)
        terms[pl.ds(2 * b, 2)] = rows.astype(BF16).reshape(2, 64, 448)

    for h in range(2):
        cross_half(0, h, 1, y)
    down_block(3)
    slot_block(mine)

    def theirs(k):
        for h in range(2):
            for r in range(2):
                if (k, h, r) in across:
                    across[k, h, r].wait_recv()
        slot_block((1 - core) * N + (y + k) % N)
        if 0 < k < N // 2:
            slot_block((1 - core) * N + (y - k + N) % N)

    for k in range(1, N // 2 + 1):
        for c, (low, size) in enumerate(SPLIT):
            for r in range(2):
                sign, far = (1 if r else -1), hops(r, c)
                index = (y - sign * k + N) % N
                if k <= far:
                    gathering[k - 1, c, r].wait_recv()
                if k < far:
                    view = unit.at[core * N + index, pl.ds(low, size)]
                    gathering[k, c, r] = remote(view, view, us.at[k, c, r], ur.at[k, c, r], on_y(sign))
                if k <= far and c % 2 == 1:
                    cross_half(k, c // 2, r, index)
        slot_block(core * N + (y + k) % N)
        if k < N // 2:
            slot_block(core * N + (y - k + N) % N)
        theirs(k - 1)
    theirs(N // 2)

    def to_tokens(g, carry):
        start = pl.multiple_of(16 * g, 16)
        rows = terms[:, pl.ds(start, 16), :].reshape(ROWS, 448)
        back = jnp.dot(place[g], rows, preferred_element_type=F32).astype(BF16)
        tok[0, pl.ds(2 * g, 2)] = back[0:256].reshape(2, N, 16, 448)
        tok[1, :, (2 * g - z + N) % N] = back[256:384].reshape(N, 16, 448)
        tok[1, :, (2 * g + 1 - z + N) % N] = back[384:512].reshape(N, 16, 448)
        return carry

    lax.fori_loop(0, GROUPS, to_tokens, 0)

    inflight = {}
    for k in range(N // 2):
        for c in range(PIECES):
            for h in range(2):
                for r in range(2):
                    sign, far = (1 if r else -1), hops(r, c)
                    view = piece(tok, h, (here[h] + sign * (far - k) + N) % N, c)
                    if 1 <= k < far:
                        inflight[k - 1, c, h, r].wait_recv()
                        view[...] = add(view[...], drecv[k - 1, c, h, r]).astype(BF16)
                    if k < far:
                        inflight[k, c, h, r] = remote(
                            view, drecv.at[k, c, h, r], ds.at[k, c, h, r], dr.at[k, c, h, r], along[h](sign)
                        )

    def up_block(b, carry):
        span = pl.ds(pl.multiple_of(b * 128, 128), 128)
        return carry + lax.dot_general(unit[b], xt[:, span], (((1,), (1,)), ((), ())), preferred_element_type=F32)

    gup_out[...] = lax.fori_loop(0, 2 * N, up_block, jnp.zeros((304, 448), F32)).astype(BF16)

    last = []
    for c in range(PIECES):
        for h in range(2):
            total = piece(tok, h, here[h], c)[...].astype(F32)
            for r in range(2):
                inflight[hops(r, c) - 1, c, h, r].wait_recv()
                total = total + drecv[hops(r, c) - 1, c, h, r].astype(F32)
            reduced[h, 2 * c:2 * c + 2] = total.astype(BF16)
            for d in (2 * c, 2 * c + 1):
                if d > 0:
                    last.append(
                        remote(reduced.at[h, d], final.at[h, d - 1], es.at[h, d - 1], er.at[h, d - 1], along[1 - h](d))
                    )
    for copy in last:
        copy.wait_recv()
    for h in range(2):
        total = reduced[h, 0].astype(F32)
        for d in range(1, N):
            total = total + final[h, d - 1].astype(F32)
        tok_out[16 * h:16 * h + 16, :] = total.astype(BF16)
    for copy in sent:
        copy.wait_send()
    for g in range(GROUPS):
        swap(g).wait_send()


def body(grad_out, probs, expert_ids, x_saved, gate_act, up_act, w_up, w_down):
    vmem, hbm = pl.BlockSpec(memory_space=pltpu.VMEM), pl.BlockSpec(memory_space=pl.ANY)
    dma = pltpu.SemaphoreType.DMA
    units, width, slots = 304, 448, 2048
    outs = pl.pallas_call(
        kernel,
        out_shape=(
            jax.ShapeDtypeStruct((TOK, width), BF16),
            jax.ShapeDtypeStruct((units, width), BF16),
            jax.ShapeDtypeStruct((units, width), BF16),
        ),
        in_specs=[hbm] * 8,
        out_specs=(vmem, vmem, vmem),
        scratch_shapes=[
            pltpu.VMEM((TOK, width), BF16),
            pltpu.VMEM((2, TOK), F32),
            pltpu.VMEM((2, TOK), jnp.int32),
            pltpu.VMEM((TOK, 512), BF16),
            pltpu.VMEM((2, N, N, 16, 512), BF16),
            pltpu.VMEM((GROUPS, ROWS, ROWS), BF16),
            pltpu.VMEM((CAP, N * N, width), BF16),
            pltpu.VMEM((CAP // 2, N * N, width), BF16),
            pltpu.VMEM((units, width), BF16),
            pltpu.VMEM((units, width), BF16),
            pltpu.VMEM((units, width), BF16),
            pltpu.VMEM((units, slots), BF16),
            pltpu.VMEM((units, slots), BF16),
            pltpu.VMEM((width, slots), BF16),
            pltpu.VMEM((N, units, 128), BF16),
            pltpu.VMEM((2 * N, units, 128), BF16),
            pltpu.VMEM((CAP, N * N, width), BF16),
            pltpu.VMEM((2, N, N, 16, width), BF16),
            pltpu.VMEM((4, PIECES, 2, 80, 128), BF16),
            pltpu.VMEM((4, PIECES, 2, 2, 2, 16, width), BF16),
            pltpu.VMEM((2, N, 16, width), BF16),
            pltpu.VMEM((2, N - 1, 16, width), BF16),
            pltpu.VMEM((units, width), F32),
            dma((8,)),
            dma((2, N - 1)), dma((2, N - 1)),
            dma((4, PIECES, 2, 2)), dma((4, PIECES, 2, 2)),
            dma((1,)), dma((1,)),
            dma((GROUPS,)), dma((GROUPS,)),
            dma((4, PIECES, 2)), dma((4, PIECES, 2)),
            dma((4, PIECES, 2)), dma((4, PIECES, 2)),
            dma((5, 2, 2)), dma((5, 2, 2)),
            dma((4, PIECES, 2, 2)), dma((4, PIECES, 2, 2)),
            dma((2, N - 1)), dma((2, N - 1)),
        ],
        compiler_params=pltpu.CompilerParams(
            collective_id=0, has_side_effects=True, vmem_limit_bytes=60 * 1024 * 1024
        ),
        cost_estimate=pl.CostEstimate(flops=4_000_000_000, bytes_accessed=8_000_000, transcendentals=0),
    )(
        grad_out,
        probs.T,
        expert_ids.T,
        jnp.swapaxes(x_saved, 1, 2),
        gate_act.T,
        up_act.T,
        w_up.T,
        w_down,
    )
    return outs[0], outs[1].T, outs[2]


def solution(mesh):
    return jax.shard_map(
        body,
        mesh=mesh,
        in_specs=(
            P("expert", "dp"),
            P("expert", None),
            P("expert", None),
            P(None, None, "dp"),
            P(None, "expert"),
            P(None, "expert"),
            P("dp", "expert"),
            P("expert", "dp"),
        ),
        out_specs=(P("expert", "dp"), P("dp", "expert"), P("expert", "dp")),
        check_vma=False,
    )
```

```python
import functools

import jax
import jax.numpy as jnp
from jax import lax
from jax.experimental import pallas as pl
from jax.experimental.pallas import tpu as pltpu
from jax.sharding import PartitionSpec as P

F32, BF16 = jnp.float32, jnp.bfloat16
MESH = pl.DeviceIdType.MESH
N = 8
TOK = 32
CAP = 32
EXPERTS = 4
GROUPS = 4
ROWS = 16 * TOK
SPLIT = ((0, 80), (80, 80), (160, 80), (240, 64))
HALVES = ((0, 160), (160, 144))
PIECES = 4


def hops(right, piece):
    return N // 2 if right == (piece < 2) else N // 2 - 1


def add(a, b):
    return a.astype(F32) + b.astype(F32)


def kernel(
    g_hbm, probs_hbm, ids_hbm, x_hbm, gate_hbm, up_hbm, wup_hbm, wdown_hbm,
    tok_out, gup_out, gdown_out,
    g_ref, probs_ref, ids_ref, shard, gath, place, routed, routed2, wdown, wdown2, wup, gate, up, xt, pair, unit, terms,
    tok, yrecv, drecv, reduced, final, total,
    ld_sem, s1, r1, s0, r0, s2, r2, ws, wr, cs, cr, ys, yr, us, ur, fs, fr, ds, dr, es, er,
):
    pos, dpos = lax.axis_index("expert"), lax.axis_index("dp")
    z, x = pos // N, pos % N
    y, core = dpos // 2, dpos % 2
    expert = pos // (N * N // EXPERTS)

    def on_x(d):
        return {"expert": z * N + (x + d + N) % N}

    def on_z(d):
        return {"expert": ((z + d + N) % N) * N + x}

    def on_y(d):
        return {"dp": ((y + d + N) % N) * 2 + core}

    other = {"dp": y * 2 + (1 - core)}
    along = (on_z, on_x)
    here = (z, x)
    sent = []

    def remote(src, dst, ssem, rsem, dev):
        copy = pltpu.make_async_remote_copy(
            src_ref=src, dst_ref=dst, send_sem=ssem, recv_sem=rsem, device_id=dev, device_id_type=MESH
        )
        copy.start()
        sent.append(copy)
        return copy

    loads = [
        pltpu.make_async_copy(g_hbm, g_ref, ld_sem.at[0]),
        pltpu.make_async_copy(probs_hbm, probs_ref, ld_sem.at[1]),
        pltpu.make_async_copy(ids_hbm, ids_ref, ld_sem.at[2]),
        pltpu.make_async_copy(wdown_hbm, wdown, ld_sem.at[3]),
        pltpu.make_async_copy(gate_hbm, gate, ld_sem.at[4]),
        pltpu.make_async_copy(up_hbm, up, ld_sem.at[5]),
        pltpu.make_async_copy(wup_hbm, wup, ld_sem.at[6]),
        pltpu.make_async_copy(x_hbm.at[expert], xt, ld_sem.at[7]),
    ]
    for load in loads:
        load.start()

    barrier = pltpu.get_barrier_semaphore()
    partners = [on_x(d) for d in range(1, N)] + [on_z(d) for d in range(1, N)] + [on_y(d) for d in (1, -1, 2, -2)] + [other]
    for dev in partners:
        pl.semaphore_signal(barrier, inc=1, device_id=dev, device_id_type=MESH)

    for load in loads[0:3]:
        load.wait()
    lane32 = lax.broadcasted_iota(jnp.int32, (TOK, TOK), 1)
    row32 = lax.broadcasted_iota(jnp.int32, (TOK, TOK), 0)
    lane128 = lax.broadcasted_iota(jnp.int32, (TOK, 128), 1)
    shard[:, 384:512] = jnp.zeros((TOK, 128), BF16)
    shard[:, 0:448] = g_ref[...]
    tail = shard[:, 384:512].astype(F32)
    for e in range(EXPERTS):
        named = ids_ref[...] == e
        prob_row = jnp.sum(jnp.where(named, probs_ref[...], 0.0), axis=0, keepdims=True)
        used_row = jnp.sum(jnp.where(named, 1.0, 0.0), axis=0, keepdims=True)
        prob = jnp.sum(jnp.where(lane32 == row32, prob_row, 0.0), axis=1, keepdims=True)
        used = jnp.sum(jnp.where(lane32 == row32, used_row, 0.0), axis=1, keepdims=True)
        before = jnp.sum(jnp.where(lane32 < row32, used_row, 0.0), axis=1, keepdims=True)
        high = prob.astype(BF16).astype(F32)
        middle = (prob - high).astype(BF16).astype(F32)
        rank = used * (before + 1.0) - 1.0
        for i, column in enumerate((high, middle, prob - high - middle, rank)):
            tail = jnp.where(lane128 == 64 + 4 * e + i, column, tail)
    shard[:, 384:512] = tail.astype(BF16)
    for h in range(2):
        gath[h, here[h], 0] = shard[16 * h:16 * h + 16, :]
    loads[3].wait()

    pl.semaphore_wait(barrier, len(partners))

    first = {}
    for d in (1, 7, 2, 6, 3, 5, 4):
        for h in range(2):
            first[h, N - d] = remote(
                gath.at[h, here[h], 0], gath.at[h, here[h], N - d], s1.at[h, d - 1], r1.at[h, N - d - 1], along[1 - h](d)
            )
    down_swap = remote(wdown, wdown2, ws.at[0], wr.at[0], other)

    def piece(ref, h, index, c):
        return ref.at[h, index, pl.ds(2 * c, 2)]

    inflight = {}
    for j in (0, 1, 7, 2, 6, 3, 5, 4):
        for h in range(2):
            if j > 0:
                first[h, j].wait_recv()
            view = gath.at[h, here[h], j]
            for r in range(2):
                inflight[h, r, j] = remote(view, view, s0.at[j, h, r], r0.at[j, h, r], along[h](1 if r else -1))
    for k in (1, 2, 3):
        for c in (0, 3, 1, 2):
            for h in range(2):
                for r in range(2):
                    sign, far = (1 if r else -1), hops(r, c)
                    if k == 1:
                        inflight[h, r, 2 * c].wait_recv()
                        inflight[h, r, 2 * c + 1].wait_recv()
                    else:
                        inflight[k - 1, c, h, r].wait_recv()
                    view = piece(gath, h, (here[h] - sign * k + N) % N, c)
                    if k == 2 and far == 4:
                        inflight[3, c, h, r] = remote(
                            view, view, s2.at[3, c, h, r], r2.at[3, c, h, r], along[h](2 * sign)
                        )
                    if k < 3:
                        inflight[k, c, h, r] = remote(
                            view, view, s2.at[k, c, h, r], r2.at[k, c, h, r], along[h](sign)
                        )
    for c in range(PIECES):
        for h in range(2):
            for r in range(2):
                if hops(r, c) == 4:
                    inflight[3, c, h, r].wait_recv()

    lane_id = lax.broadcasted_iota(jnp.int32, (ROWS, ROWS), 1)
    row_id = lax.broadcasted_iota(jnp.int32, (ROWS, 1), 0)
    tile = (row_id % 256) // 16
    source = jnp.where(
        row_id < 256, (tile // 8) * 8 + (tile % 8 + x) % 8, (tile // 8) * 8 + tile % 8
    )
    tail_lane = lax.broadcasted_iota(jnp.int32, (ROWS, 128), 1) - 64 - 4 * expert

    def swap(g):
        span = pl.ds(pl.multiple_of(16 * g, 16), 16)
        return pltpu.make_async_remote_copy(
            src_ref=routed.at[pl.ds((1 - core) * 16, 16), span], dst_ref=routed2.at[:, span],
            send_sem=cs.at[g], recv_sem=cr.at[g], device_id=other, device_id_type=MESH,
        )

    def to_slots(g, carry):
        one = gath[0, pl.ds(2 * g, 2)].reshape(256, 512)
        two = gath[1, :, (2 * g - z + N) % N].reshape(128, 512)
        three = gath[1, :, (2 * g + 1 - z + N) % N].reshape(128, 512)
        rows = jnp.concatenate([one, two, three], axis=0)
        extra = rows[:, 384:512].astype(F32)
        weight = jnp.sum(jnp.where((tail_lane >= 0) & (tail_lane < 3), extra, 0.0), axis=1, keepdims=True)
        rank = jnp.sum(jnp.where(tail_lane == 3, extra, 0.0), axis=1, keepdims=True)
        key = rank.astype(jnp.int32) * 16 + source
        onehot = jnp.where(key == lane_id, 1.0, 0.0).astype(BF16)
        place[g] = onehot
        scaled = (rows.astype(F32) * weight).astype(BF16)
        moved = lax.dot_general(onehot, scaled, (((0,), (0,)), ((), ())), preferred_element_type=F32)
        start = pl.multiple_of(16 * g, 16)
        routed[:, pl.ds(start, 16), :] = moved[:, 0:448].astype(BF16).reshape(CAP, 16, 448)
        swap(g).start()
        return carry

    lax.fori_loop(0, GROUPS, to_slots, 0)

    down_swap.wait_recv()
    for g in range(GROUPS):
        swap(g).wait_recv()

    def partial(offset, count):
        def step(n, carry):
            i = (y + offset + N + n) % N
            mine = routed[pl.ds(core * 16 + 2 * i, 2)].reshape(128, 448)
            theirs = routed2[pl.ds(2 * i, 2)].reshape(128, 448)
            dims = (((1,), (1,)), ((), ()))
            pair[i] = (
                lax.dot_general(wdown[...], mine, dims, preferred_element_type=F32)
                + lax.dot_general(wdown2[...], theirs, dims, preferred_element_type=F32)
            ).astype(BF16)
            return carry

        lax.fori_loop(0, count, step, 0)

    def down_blocks(low):
        def step(b, carry):
            span = pl.ds(pl.multiple_of(512 * b, 512), 512)
            hidden = (gate[:, span].astype(F32) * up[:, span].astype(F32)).astype(BF16)
            rows = routed[pl.ds(8 * b, 8)].reshape(512, 448)
            total[...] += jnp.dot(hidden, rows, preferred_element_type=F32)
            return carry

        lax.fori_loop(low, low + 2, step, 0)

    def ring_start(far, sign, view, recv, ssem, rsem, dev):
        copies = {}
        if far == 4:
            copies[0] = remote(view(4 * sign), recv(0), ssem(0), rsem(0), dev(2 * sign))
        copies[far - 3] = remote(view(3 * sign), recv(far - 3), ssem(far - 3), rsem(far - 3), dev(sign))
        return copies

    def ring_step(stage, copies, far, sign, view, recv, ssem, rsem, dev):
        own = view((3 - stage) * sign)
        value = own[...].astype(F32)
        for i in (0, 1) if (far, stage) == (4, 1) else (far + stage - 4,):
            copies[i].wait_recv()
            value = value + recv(i)[...].astype(F32)
        own[...] = value.astype(BF16)
        n = far + stage - 3
        copies[n] = remote(own, recv(n), ssem(n), rsem(n), dev(sign))

    def y_ring(c, r):
        low, size = SPLIT[c]
        return (
            hops(r, c),
            1 if r else -1,
            lambda offset: pair.at[(y + offset + N) % N, pl.ds(low, size)],
            lambda i: yrecv.at[i, c, r, pl.ds(0, size)],
            lambda i: ys.at[i, c, r],
            lambda i: yr.at[i, c, r],
            on_y,
        )

    inflight = {}
    partial(3, 3)
    for c in range(PIECES):
        for r in range(2):
            inflight[c, r] = ring_start(*y_ring(c, r))
    partial(-2, 5)
    total[...] = jnp.zeros_like(total)
    for load in loads[4:6]:
        load.wait()
    for stage in (1, 2):
        for c in range(PIECES):
            for r in range(2):
                ring_step(stage, inflight[c, r], *y_ring(c, r))
        down_blocks(2 * stage - 2)
    for load in loads[6:]:
        load.wait()

    mine = core * N + y
    lanes = pl.ds(pl.multiple_of(mine * 128, 128), 128)
    gathering = {}
    for c, (low, size) in enumerate(SPLIT):
        whole = pair[y, low:low + size].astype(F32)
        for r in range(2):
            inflight[c, r][hops(r, c) - 1].wait_recv()
            whole = whole + yrecv[hops(r, c) - 1, c, r, 0:size].astype(F32)
        unit[mine, low:low + size] = (whole * gate[low:low + size, lanes].astype(F32)).astype(BF16)
        view = unit.at[mine, pl.ds(low, size)]
        for r in range(2):
            gathering[0, c, r] = remote(view, view, us.at[0, c, r], ur.at[0, c, r], on_y(1 if r else -1))
    across = {}

    def cross_half(k, h, r, index):
        view = unit.at[core * N + index, pl.ds(HALVES[h][0], HALVES[h][1])]
        across[k, h, r] = remote(view, view, fs.at[k, h, r], fr.at[k, h, r], other)

    def slot_blocks(owner, offset, stride, count):
        def step(n, carry):
            b = owner * N + (y + offset + N + stride * n) % N
            rows = lax.dot_general(unit[b], wup[...], (((0,), (0,)), ((), ())), preferred_element_type=F32)
            terms[pl.ds(2 * b, 2)] = rows.astype(BF16).reshape(2, 64, 448)
            return carry

        lax.fori_loop(0, count, step, 0)

    def arrived(k):
        for h in range(2):
            for r in range(2):
                if (k, h, r) in across:
                    across[k, h, r].wait_recv()

    for h in range(2):
        cross_half(0, h, 1, y)
    gdown_out[...] = total[...].astype(BF16)
    slot_blocks(core, 0, 1, 1)
    for k in (1, 2, 3):
        for c, (low, size) in enumerate(SPLIT):
            for r in range(2):
                sign, far = (1 if r else -1), hops(r, c)
                index = (y - sign * k + N) % N
                gathering[k - 1, c, r].wait_recv()
                view = unit.at[core * N + index, pl.ds(low, size)]
                if k == 2 and far == 4:
                    gathering[3, c, r] = remote(view, view, us.at[3, c, r], ur.at[3, c, r], on_y(2 * sign))
                if k < 3:
                    gathering[k, c, r] = remote(view, view, us.at[k, c, r], ur.at[k, c, r], on_y(sign))
                if c % 2 == 1:
                    cross_half(k, c // 2, r, index)
        if k < 3:
            slot_blocks(core, -k, 2 * k, 2)
            arrived(k - 1)
            slot_blocks(1 - core, 1 - k, 2 * k - 2, min(k, 2))
    for c in range(PIECES):
        for r in range(2):
            if hops(r, c) == 4:
                gathering[3, c, r].wait_recv()
                if c % 2 == 1:
                    cross_half(4, c // 2, r, (y + 4) % N)
    slot_blocks(core, 3, 1, 3)
    arrived(2)
    slot_blocks(1 - core, -2, 4, 2)
    arrived(3)
    arrived(4)
    slot_blocks(1 - core, 3, 1, 3)
    total[...] = jnp.zeros_like(total)

    def to_tokens(g, carry):
        start = pl.multiple_of(16 * g, 16)
        rows = terms[:, pl.ds(start, 16), :].reshape(ROWS, 448)
        back = jnp.dot(place[g], rows, preferred_element_type=F32).astype(BF16)
        tok[0, pl.ds(2 * g, 2)] = back[0:256].reshape(2, N, 16, 448)
        tok[1, :, (2 * g - z + N) % N] = back[256:384].reshape(N, 16, 448)
        tok[1, :, (2 * g + 1 - z + N) % N] = back[384:512].reshape(N, 16, 448)
        return carry

    lax.fori_loop(0, GROUPS, to_tokens, 0)

    def token_ring(c, h, r):
        return (
            hops(r, c),
            1 if r else -1,
            lambda offset: piece(tok, h, (here[h] + offset + N) % N, c),
            lambda i: drecv.at[i, c, h, r],
            lambda i: ds.at[i, c, h, r],
            lambda i: dr.at[i, c, h, r],
            along[h],
        )

    def up_blocks(low, count):
        def step(b, carry):
            span = pl.ds(pl.multiple_of(b * 128, 128), 128)
            total[...] += lax.dot_general(
                unit[b], xt[:, span], (((1,), (1,)), ((), ())), preferred_element_type=F32
            )
            return carry

        lax.fori_loop(low, low + count, step, 0)

    inflight = {}
    for stage in range(3):
        for c in range(PIECES):
            for h in range(2):
                for r in range(2):
                    if stage == 0:
                        inflight[c, h, r] = ring_start(*token_ring(c, h, r))
                    else:
                        ring_step(stage, inflight[c, h, r], *token_ring(c, h, r))
        up_blocks((0, 6, 11)[stage], (6, 5, 5)[stage])
    gup_out[...] = total[...].astype(BF16)

    last = []
    for c in range(PIECES):
        for h in range(2):
            whole = piece(tok, h, here[h], c)[...].astype(F32)
            for r in range(2):
                inflight[c, h, r][hops(r, c) - 1].wait_recv()
                whole = whole + drecv[hops(r, c) - 1, c, h, r].astype(F32)
            reduced[h, 2 * c:2 * c + 2] = whole.astype(BF16)
            for d in (2 * c, 2 * c + 1):
                if d > 0:
                    last.append(
                        remote(reduced.at[h, d], final.at[h, d - 1], es.at[h, d - 1], er.at[h, d - 1], along[1 - h](d))
                    )
    for copy in last:
        copy.wait_recv()
    for h in range(2):
        whole = reduced[h, 0].astype(F32)
        for d in range(1, N):
            whole = whole + final[h, d - 1].astype(F32)
        tok_out[16 * h:16 * h + 16, :] = whole.astype(BF16)
    for copy in sent:
        copy.wait_send()
    for g in range(GROUPS):
        swap(g).wait_send()


def body(grad_out, probs, expert_ids, x_saved, gate_act, up_act, w_up, w_down):
    vmem, hbm = pl.BlockSpec(memory_space=pltpu.VMEM), pl.BlockSpec(memory_space=pl.ANY)
    dma = pltpu.SemaphoreType.DMA
    units, width, slots = 304, 448, 2048
    outs = pl.pallas_call(
        kernel,
        out_shape=(
            jax.ShapeDtypeStruct((TOK, width), BF16),
            jax.ShapeDtypeStruct((units, width), BF16),
            jax.ShapeDtypeStruct((units, width), BF16),
        ),
        in_specs=[hbm] * 8,
        out_specs=(vmem, vmem, vmem),
        scratch_shapes=[
            pltpu.VMEM((TOK, width), BF16),
            pltpu.VMEM((2, TOK), F32),
            pltpu.VMEM((2, TOK), jnp.int32),
            pltpu.VMEM((TOK, 512), BF16),
            pltpu.VMEM((2, N, N, 16, 512), BF16),
            pltpu.VMEM((GROUPS, ROWS, ROWS), BF16),
            pltpu.VMEM((CAP, N * N, width), BF16),
            pltpu.VMEM((CAP // 2, N * N, width), BF16),
            pltpu.VMEM((units, width), BF16),
            pltpu.VMEM((units, width), BF16),
            pltpu.VMEM((units, width), BF16),
            pltpu.VMEM((units, slots), BF16),
            pltpu.VMEM((units, slots), BF16),
            pltpu.VMEM((width, slots), BF16),
            pltpu.VMEM((N, units, 128), BF16),
            pltpu.VMEM((2 * N, units, 128), BF16),
            pltpu.VMEM((CAP, N * N, width), BF16),
            pltpu.VMEM((2, N, N, 16, width), BF16),
            pltpu.VMEM((4, PIECES, 2, 80, 128), BF16),
            pltpu.VMEM((4, PIECES, 2, 2, 2, 16, width), BF16),
            pltpu.VMEM((2, N, 16, width), BF16),
            pltpu.VMEM((2, N - 1, 16, width), BF16),
            pltpu.VMEM((units, width), F32),
            dma((8,)),
            dma((2, N - 1)), dma((2, N - 1)),
            dma((N, 2, 2)), dma((N, 2, 2)),
            dma((4, PIECES, 2, 2)), dma((4, PIECES, 2, 2)),
            dma((1,)), dma((1,)),
            dma((GROUPS,)), dma((GROUPS,)),
            dma((4, PIECES, 2)), dma((4, PIECES, 2)),
            dma((4, PIECES, 2)), dma((4, PIECES, 2)),
            dma((5, 2, 2)), dma((5, 2, 2)),
            dma((4, PIECES, 2, 2)), dma((4, PIECES, 2, 2)),
            dma((2, N - 1)), dma((2, N - 1)),
        ],
        compiler_params=pltpu.CompilerParams(
            collective_id=0, has_side_effects=True, vmem_limit_bytes=60 * 1024 * 1024
        ),
        cost_estimate=pl.CostEstimate(flops=4_000_000_000, bytes_accessed=8_000_000, transcendentals=0),
    )(
        grad_out,
        probs.T,
        expert_ids.T,
        jnp.swapaxes(x_saved, 1, 2),
        gate_act.T,
        up_act.T,
        w_up.T,
        w_down,
    )
    return outs[0], outs[1].T, outs[2]


def solution(mesh):
    return jax.shard_map(
        body,
        mesh=mesh,
        in_specs=(
            P("expert", "dp"),
            P("expert", None),
            P("expert", None),
            P(None, None, "dp"),
            P(None, "expert"),
            P(None, "expert"),
            P("dp", "expert"),
            P("expert", "dp"),
        ),
        out_specs=(P("expert", "dp"), P("dp", "expert"), P("expert", "dp")),
        check_vma=False,
    )
```

```python
import functools

import jax
import jax.numpy as jnp
from jax import lax
from jax.experimental import pallas as pl
from jax.experimental.pallas import tpu as pltpu
from jax.sharding import PartitionSpec as P

F32, BF16 = jnp.float32, jnp.bfloat16
MESH = pl.DeviceIdType.MESH
N = 8
TOK = 32
CAP = 32
EXPERTS = 4
GROUPS = 4
ROWS = 16 * TOK
SPLIT = ((0, 80), (80, 80), (160, 80), (240, 64))
HALVES = ((0, 160), (160, 144))
PIECES = 4


def hops(right, piece):
    return N // 2 if right == (piece < 2) else N // 2 - 1


def add(a, b):
    return a.astype(F32) + b.astype(F32)


def kernel(
    g_hbm, probs_hbm, ids_hbm, x_hbm, gate_hbm, up_hbm, wup_hbm, wdown_hbm,
    tok_out, gup_out, gdown_out,
    g_ref, probs_ref, ids_ref, shard, gath, place, scaled, routed, routed2, wdown, wdown2, wup, gate, up, xt, pair, unit, terms,
    tok, yrecv, drecv, reduced, final, total,
    ld_sem, s1, r1, s0, r0, s2, r2, ws, wr, cs, cr, ys, yr, us, ur, fs, fr, ds, dr, es, er,
):
    pos, dpos = lax.axis_index("expert"), lax.axis_index("dp")
    z, x = pos // N, pos % N
    y, core = dpos // 2, dpos % 2
    expert = pos // (N * N // EXPERTS)

    def on_x(d):
        return {"expert": z * N + (x + d + N) % N}

    def on_z(d):
        return {"expert": ((z + d + N) % N) * N + x}

    def on_y(d):
        return {"dp": ((y + d + N) % N) * 2 + core}

    other = {"dp": y * 2 + (1 - core)}
    along = (on_z, on_x)
    here = (z, x)
    sent = []

    def remote(src, dst, ssem, rsem, dev):
        copy = pltpu.make_async_remote_copy(
            src_ref=src, dst_ref=dst, send_sem=ssem, recv_sem=rsem, device_id=dev, device_id_type=MESH
        )
        copy.start()
        sent.append(copy)
        return copy

    loads = [
        pltpu.make_async_copy(g_hbm, g_ref, ld_sem.at[0]),
        pltpu.make_async_copy(probs_hbm, probs_ref, ld_sem.at[1]),
        pltpu.make_async_copy(ids_hbm, ids_ref, ld_sem.at[2]),
        pltpu.make_async_copy(wdown_hbm, wdown, ld_sem.at[3]),
        pltpu.make_async_copy(gate_hbm, gate, ld_sem.at[4]),
        pltpu.make_async_copy(up_hbm, up, ld_sem.at[5]),
        pltpu.make_async_copy(wup_hbm, wup, ld_sem.at[6]),
        pltpu.make_async_copy(x_hbm.at[expert], xt, ld_sem.at[7]),
    ]
    for load in loads:
        load.start()

    barrier = pltpu.get_barrier_semaphore()
    partners = [on_x(d) for d in range(1, N)] + [on_z(d) for d in range(1, N)] + [on_y(d) for d in (1, -1, 2, -2)] + [other]
    for dev in partners:
        pl.semaphore_signal(barrier, inc=1, device_id=dev, device_id_type=MESH)

    for load in loads[0:3]:
        load.wait()
    lane32 = lax.broadcasted_iota(jnp.int32, (TOK, TOK), 1)
    row32 = lax.broadcasted_iota(jnp.int32, (TOK, TOK), 0)
    lane128 = lax.broadcasted_iota(jnp.int32, (TOK, 128), 1)
    shard[:, 384:512] = jnp.zeros((TOK, 128), BF16)
    shard[:, 0:448] = g_ref[...]
    tail = shard[:, 384:512].astype(F32)
    def column(row):
        return jnp.sum(jnp.where(lane32 == row32, row, 0.0), axis=1, keepdims=True)

    ids = ids_ref[...].astype(F32)
    expert_of_lane = ((lane128 - 64) // 4).astype(F32)
    ones = column(ids[0:1]) == expert_of_lane
    twos = column(ids[1:2]) == expert_of_lane
    prob = jnp.where(ones, column(probs_ref[0:1]), 0.0) + jnp.where(twos, column(probs_ref[1:2]), 0.0)
    used = jnp.where(ones, 1.0, 0.0) + jnp.where(twos, 1.0, 0.0)
    lower = jnp.where(lane32 < row32, 1.0, 0.0).astype(BF16)
    before = jnp.dot(lower, used.astype(BF16), preferred_element_type=F32)
    high = prob.astype(BF16).astype(F32)
    middle = (prob - high).astype(BF16).astype(F32)
    kind = lane128 % 4
    extra = jnp.where(kind == 0, high, jnp.where(kind == 1, middle, prob - high - middle))
    extra = jnp.where(kind == 3, used * (before + 1.0) - 1.0, extra)
    tail = jnp.where(lane128 >= 64, extra, tail)
    shard[:, 384:512] = tail.astype(BF16)
    for h in range(2):
        gath[h, here[h], 0] = shard[16 * h:16 * h + 16, :]

    pl.semaphore_wait(barrier, len(partners))

    first = {}
    for d in (1, 7, 2, 6, 3, 5, 4):
        for h in range(2):
            first[h, N - d] = remote(
                gath.at[h, here[h], 0], gath.at[h, here[h], N - d], s1.at[h, d - 1], r1.at[h, N - d - 1], along[1 - h](d)
            )
    loads[3].wait()
    down_swap = remote(wdown, wdown2, ws.at[0], wr.at[0], other)

    def piece(ref, h, index, c):
        return ref.at[h, index, pl.ds(2 * c, 2)]

    inflight = {}
    for j in (0, 1, 7, 2, 6, 3, 5, 4):
        for h in range(2):
            if j > 0:
                first[h, j].wait_recv()
            view = gath.at[h, here[h], j]
            for r in range(2):
                inflight[h, r, j] = remote(view, view, s0.at[j, h, r], r0.at[j, h, r], along[h](1 if r else -1))
    for k in (1, 2):
        for c in (0, 3, 1, 2):
            for h in range(2):
                for r in range(2):
                    sign, far = (1 if r else -1), hops(r, c)
                    if k == 1:
                        inflight[h, r, 2 * c].wait_recv()
                        inflight[h, r, 2 * c + 1].wait_recv()
                    else:
                        inflight[k - 1, c, h, r].wait_recv()
                    view = piece(gath, h, (here[h] - sign * k + N) % N, c)
                    if k == 2 and far == 4:
                        inflight[3, c, h, r] = remote(
                            view, view, s2.at[3, c, h, r], r2.at[3, c, h, r], along[h](2 * sign)
                        )
                    inflight[k, c, h, r] = remote(
                        view, view, s2.at[k, c, h, r], r2.at[k, c, h, r], along[h](sign)
                    )

    lane_id = lax.broadcasted_iota(jnp.int32, (128, ROWS), 1)
    step_id = lax.broadcasted_iota(jnp.int32, (128, 1), 0) // 16
    tail_lane = lax.broadcasted_iota(jnp.int32, (128, 128), 1) - 64 - 4 * expert

    def onehot_and_scaled(rows, source):
        extra = rows[:, 384:512].astype(F32)
        weight = jnp.sum(jnp.where((tail_lane >= 0) & (tail_lane < 3), extra, 0.0), axis=1, keepdims=True)
        rank = jnp.sum(jnp.where(tail_lane == 3, extra, 0.0), axis=1, keepdims=True)
        key = rank.astype(jnp.int32) * 16 + source
        return jnp.where(key == lane_id, 1.0, 0.0).astype(BF16), (rows.astype(F32) * weight).astype(BF16)

    def planes(offset, stride, count):
        def step(n, carry):
            zz = (z + offset + N + stride * n) % N
            xx = (x + offset + N + stride * n) % N
            low = pl.ds(pl.multiple_of((zz % 2) * 128, 128), 128)
            onehot, rows = onehot_and_scaled(
                gath[0, zz].reshape(128, 512), (zz % 2) * 8 + (x + step_id) % 8
            )
            place[zz // 2, low] = onehot
            scaled[zz // 2, low] = rows
            onehot, rows = onehot_and_scaled(
                gath[1, xx].reshape(128, 512), ((z + step_id) % 2) * 8 + xx
            )
            for j in range(N):
                zj = (z + j) % N
                at = pl.ds(pl.multiple_of(256 + (zj % 2) * 128 + xx * 16, 16), 16)
                place[zj // 2, at] = onehot[16 * j:16 * j + 16]
                scaled[zj // 2, at] = rows[16 * j:16 * j + 16]
            return carry

        lax.fori_loop(0, count, step, 0)

    planes(-2, 1, 5)
    for c in range(PIECES):
        for h in range(2):
            for r in range(2):
                inflight[2, c, h, r].wait_recv()
                if hops(r, c) == 4:
                    inflight[3, c, h, r].wait_recv()
    planes(3, 1, 3)

    def swap(g):
        span = pl.ds(pl.multiple_of(16 * g, 16), 16)
        return pltpu.make_async_remote_copy(
            src_ref=routed.at[pl.ds((1 - core) * 16, 16), span], dst_ref=routed2.at[:, span],
            send_sem=cs.at[g], recv_sem=cr.at[g], device_id=other, device_id_type=MESH,
        )

    def to_slots(g, carry):
        moved = lax.dot_general(place[g], scaled[g], (((0,), (0,)), ((), ())), preferred_element_type=F32)
        start = pl.multiple_of(16 * g, 16)
        routed[:, pl.ds(start, 16), :] = moved[:, 0:448].astype(BF16).reshape(CAP, 16, 448)
        swap(g).start()
        return carry

    lax.fori_loop(0, GROUPS, to_slots, 0)

    down_swap.wait_recv()
    for g in range(GROUPS):
        swap(g).wait_recv()

    def partial(offset, count):
        def step(n, carry):
            i = (y + offset + N + n) % N
            mine = routed[pl.ds(core * 16 + 2 * i, 2)].reshape(128, 448)
            theirs = routed2[pl.ds(2 * i, 2)].reshape(128, 448)
            dims = (((1,), (1,)), ((), ()))
            pair[i] = (
                lax.dot_general(wdown[...], mine, dims, preferred_element_type=F32)
                + lax.dot_general(wdown2[...], theirs, dims, preferred_element_type=F32)
            ).astype(BF16)
            return carry

        lax.fori_loop(0, count, step, 0)

    def down_blocks(low):
        def step(b, carry):
            span = pl.ds(pl.multiple_of(512 * b, 512), 512)
            hidden = (gate[:, span].astype(F32) * up[:, span].astype(F32)).astype(BF16)
            rows = routed[pl.ds(8 * b, 8)].reshape(512, 448)
            total[...] += jnp.dot(hidden, rows, preferred_element_type=F32)
            return carry

        lax.fori_loop(low, low + 2, step, 0)

    def ring_start(far, sign, view, recv, ssem, rsem, dev):
        copies = {}
        if far == 4:
            copies[0] = remote(view(4 * sign), recv(0), ssem(0), rsem(0), dev(2 * sign))
        copies[far - 3] = remote(view(3 * sign), recv(far - 3), ssem(far - 3), rsem(far - 3), dev(sign))
        return copies

    def ring_step(stage, copies, far, sign, view, recv, ssem, rsem, dev):
        own = view((3 - stage) * sign)
        value = own[...].astype(F32)
        for i in (0, 1) if (far, stage) == (4, 1) else (far + stage - 4,):
            copies[i].wait_recv()
            value = value + recv(i)[...].astype(F32)
        own[...] = value.astype(BF16)
        n = far + stage - 3
        copies[n] = remote(own, recv(n), ssem(n), rsem(n), dev(sign))

    def y_ring(c, r):
        low, size = SPLIT[c]
        return (
            hops(r, c),
            1 if r else -1,
            lambda offset: pair.at[(y + offset + N) % N, pl.ds(low, size)],
            lambda i: yrecv.at[i, c, r, pl.ds(0, size)],
            lambda i: ys.at[i, c, r],
            lambda i: yr.at[i, c, r],
            on_y,
        )

    inflight = {}
    partial(3, 3)
    for c in range(PIECES):
        for r in range(2):
            inflight[c, r] = ring_start(*y_ring(c, r))
    partial(-2, 5)
    total[...] = jnp.zeros_like(total)
    for load in loads[4:6]:
        load.wait()
    for stage in (1, 2):
        for c in range(PIECES):
            for r in range(2):
                ring_step(stage, inflight[c, r], *y_ring(c, r))
        down_blocks(2 * stage - 2)
    for load in loads[6:]:
        load.wait()

    mine = core * N + y
    lanes = pl.ds(pl.multiple_of(mine * 128, 128), 128)
    gathering = {}
    for c, (low, size) in enumerate(SPLIT):
        whole = pair[y, low:low + size].astype(F32)
        for r in range(2):
            inflight[c, r][hops(r, c) - 1].wait_recv()
            whole = whole + yrecv[hops(r, c) - 1, c, r, 0:size].astype(F32)
        unit[mine, low:low + size] = (whole * gate[low:low + size, lanes].astype(F32)).astype(BF16)
        view = unit.at[mine, pl.ds(low, size)]
        for r in range(2):
            gathering[0, c, r] = remote(view, view, us.at[0, c, r], ur.at[0, c, r], on_y(1 if r else -1))
    across = {}

    def cross_half(k, h, r, index):
        view = unit.at[core * N + index, pl.ds(HALVES[h][0], HALVES[h][1])]
        across[k, h, r] = remote(view, view, fs.at[k, h, r], fr.at[k, h, r], other)

    def slot_blocks(owner, offset, stride, count):
        def step(n, carry):
            b = owner * N + (y + offset + N + stride * n) % N
            rows = lax.dot_general(unit[b], wup[...], (((0,), (0,)), ((), ())), preferred_element_type=F32)
            terms[pl.ds(2 * b, 2)] = rows.astype(BF16).reshape(2, 64, 448)
            return carry

        lax.fori_loop(0, count, step, 0)

    def arrived(k):
        for h in range(2):
            for r in range(2):
                if (k, h, r) in across:
                    across[k, h, r].wait_recv()

    for h in range(2):
        cross_half(0, h, 1, y)
    gdown_out[...] = total[...].astype(BF16)
    slot_blocks(core, 0, 1, 1)
    for k in (1, 2, 3):
        for c, (low, size) in enumerate(SPLIT):
            for r in range(2):
                sign, far = (1 if r else -1), hops(r, c)
                index = (y - sign * k + N) % N
                gathering[k - 1, c, r].wait_recv()
                view = unit.at[core * N + index, pl.ds(low, size)]
                if k == 2 and far == 4:
                    gathering[3, c, r] = remote(view, view, us.at[3, c, r], ur.at[3, c, r], on_y(2 * sign))
                if k < 3:
                    gathering[k, c, r] = remote(view, view, us.at[k, c, r], ur.at[k, c, r], on_y(sign))
                if c % 2 == 1:
                    cross_half(k, c // 2, r, index)
        if k < 3:
            slot_blocks(core, -k, 2 * k, 2)
            arrived(k - 1)
            slot_blocks(1 - core, 1 - k, 2 * k - 2, min(k, 2))
    for c in range(PIECES):
        for r in range(2):
            if hops(r, c) == 4:
                gathering[3, c, r].wait_recv()
                if c % 2 == 1:
                    cross_half(4, c // 2, r, (y + 4) % N)
    slot_blocks(core, 3, 1, 3)
    arrived(2)
    slot_blocks(1 - core, -2, 4, 2)
    arrived(3)
    arrived(4)
    slot_blocks(1 - core, 3, 1, 3)
    total[...] = jnp.zeros_like(total)

    def to_tokens(g, carry):
        start = pl.multiple_of(16 * g, 16)
        rows = terms[:, pl.ds(start, 16), :].reshape(ROWS, 448)
        back = jnp.dot(place[g], rows, preferred_element_type=F32).astype(BF16)
        tok[0, pl.ds(2 * g, 2)] = back[0:256].reshape(2, N, 16, 448)
        tok[1, :, (2 * g - z + N) % N] = back[256:384].reshape(N, 16, 448)
        tok[1, :, (2 * g + 1 - z + N) % N] = back[384:512].reshape(N, 16, 448)
        return carry

    lax.fori_loop(0, GROUPS, to_tokens, 0)

    def token_ring(c, h, r):
        return (
            hops(r, c),
            1 if r else -1,
            lambda offset: piece(tok, h, (here[h] + offset + N) % N, c),
            lambda i: drecv.at[i, c, h, r],
            lambda i: ds.at[i, c, h, r],
            lambda i: dr.at[i, c, h, r],
            along[h],
        )

    def up_blocks(low, count):
        def step(b, carry):
            span = pl.ds(pl.multiple_of(b * 128, 128), 128)
            total[...] += lax.dot_general(
                unit[b], xt[:, span], (((1,), (1,)), ((), ())), preferred_element_type=F32
            )
            return carry

        lax.fori_loop(low, low + count, step, 0)

    inflight = {}
    for stage in range(3):
        for c in range(PIECES):
            for h in range(2):
                for r in range(2):
                    if stage == 0:
                        inflight[c, h, r] = ring_start(*token_ring(c, h, r))
                    else:
                        ring_step(stage, inflight[c, h, r], *token_ring(c, h, r))
        up_blocks((0, 6, 11)[stage], (6, 5, 5)[stage])
    gup_out[...] = total[...].astype(BF16)

    last = []
    for c in range(PIECES):
        for h in range(2):
            whole = piece(tok, h, here[h], c)[...].astype(F32)
            for r in range(2):
                inflight[c, h, r][hops(r, c) - 1].wait_recv()
                whole = whole + drecv[hops(r, c) - 1, c, h, r].astype(F32)
            reduced[h, 2 * c:2 * c + 2] = whole.astype(BF16)
            for d in (2 * c, 2 * c + 1):
                if d > 0:
                    last.append(
                        remote(reduced.at[h, d], final.at[h, d - 1], es.at[h, d - 1], er.at[h, d - 1], along[1 - h](d))
                    )
    for copy in last:
        copy.wait_recv()
    for h in range(2):
        whole = reduced[h, 0].astype(F32)
        for d in range(1, N):
            whole = whole + final[h, d - 1].astype(F32)
        tok_out[16 * h:16 * h + 16, :] = whole.astype(BF16)
    for copy in sent:
        copy.wait_send()
    for g in range(GROUPS):
        swap(g).wait_send()


def body(grad_out, probs, expert_ids, x_saved, gate_act, up_act, w_up, w_down):
    vmem, hbm = pl.BlockSpec(memory_space=pltpu.VMEM), pl.BlockSpec(memory_space=pl.ANY)
    dma = pltpu.SemaphoreType.DMA
    units, width, slots = 304, 448, 2048
    outs = pl.pallas_call(
        kernel,
        out_shape=(
            jax.ShapeDtypeStruct((TOK, width), BF16),
            jax.ShapeDtypeStruct((units, width), BF16),
            jax.ShapeDtypeStruct((units, width), BF16),
        ),
        in_specs=[hbm] * 8,
        out_specs=(vmem, vmem, vmem),
        scratch_shapes=[
            pltpu.VMEM((TOK, width), BF16),
            pltpu.VMEM((2, TOK), F32),
            pltpu.VMEM((2, TOK), jnp.int32),
            pltpu.VMEM((TOK, 512), BF16),
            pltpu.VMEM((2, N, N, 16, 512), BF16),
            pltpu.VMEM((GROUPS, ROWS, ROWS), BF16),
            pltpu.VMEM((GROUPS, ROWS, 512), BF16),
            pltpu.VMEM((CAP, N * N, width), BF16),
            pltpu.VMEM((CAP // 2, N * N, width), BF16),
            pltpu.VMEM((units, width), BF16),
            pltpu.VMEM((units, width), BF16),
            pltpu.VMEM((units, width), BF16),
            pltpu.VMEM((units, slots), BF16),
            pltpu.VMEM((units, slots), BF16),
            pltpu.VMEM((width, slots), BF16),
            pltpu.VMEM((N, units, 128), BF16),
            pltpu.VMEM((2 * N, units, 128), BF16),
            pltpu.VMEM((CAP, N * N, width), BF16),
            pltpu.VMEM((2, N, N, 16, width), BF16),
            pltpu.VMEM((4, PIECES, 2, 80, 128), BF16),
            pltpu.VMEM((4, PIECES, 2, 2, 2, 16, width), BF16),
            pltpu.VMEM((2, N, 16, width), BF16),
            pltpu.VMEM((2, N - 1, 16, width), BF16),
            pltpu.VMEM((units, width), F32),
            dma((8,)),
            dma((2, N - 1)), dma((2, N - 1)),
            dma((N, 2, 2)), dma((N, 2, 2)),
            dma((4, PIECES, 2, 2)), dma((4, PIECES, 2, 2)),
            dma((1,)), dma((1,)),
            dma((GROUPS,)), dma((GROUPS,)),
            dma((4, PIECES, 2)), dma((4, PIECES, 2)),
            dma((4, PIECES, 2)), dma((4, PIECES, 2)),
            dma((5, 2, 2)), dma((5, 2, 2)),
            dma((4, PIECES, 2, 2)), dma((4, PIECES, 2, 2)),
            dma((2, N - 1)), dma((2, N - 1)),
        ],
        compiler_params=pltpu.CompilerParams(
            collective_id=0, has_side_effects=True, vmem_limit_bytes=60 * 1024 * 1024
        ),
        cost_estimate=pl.CostEstimate(flops=4_000_000_000, bytes_accessed=8_000_000, transcendentals=0),
    )(
        grad_out,
        probs.T,
        expert_ids.T,
        jnp.swapaxes(x_saved, 1, 2),
        gate_act.T,
        up_act.T,
        w_up.T,
        w_down,
    )
    return outs[0], outs[1].T, outs[2]


def solution(mesh):
    return jax.shard_map(
        body,
        mesh=mesh,
        in_specs=(
            P("expert", "dp"),
            P("expert", None),
            P("expert", None),
            P(None, None, "dp"),
            P(None, "expert"),
            P(None, "expert"),
            P("dp", "expert"),
            P("expert", "dp"),
        ),
        out_specs=(P("expert", "dp"), P("dp", "expert"), P("expert", "dp")),
        check_vma=False,
    )
```

```python
import functools

import jax
import jax.numpy as jnp
from jax import lax
from jax.experimental import pallas as pl
from jax.experimental.pallas import tpu as pltpu
from jax.sharding import PartitionSpec as P

F32, BF16 = jnp.float32, jnp.bfloat16
MESH = pl.DeviceIdType.MESH
N = 8
TOK = 32
CAP = 32
EXPERTS = 4
GROUPS = 4
ROWS = 16 * TOK
SPLIT = ((0, 80), (80, 80), (160, 80), (240, 64))
HALVES = ((0, 160), (160, 144))
PIECES = 4


def hops(right, piece):
    return N // 2 if right == (piece < 2) else N // 2 - 1


def add(a, b):
    return a.astype(F32) + b.astype(F32)


def kernel(
    g_hbm, probs_hbm, ids_hbm, x_hbm, gate_hbm, up_hbm, wup_hbm, wdown_hbm,
    tok_out, gup_out, gdown_out,
    g_ref, probs_ref, ids_ref, shard, gath, place, scaled, routed, routed2, wdown, wdown2, wup, gate, up, xt, pair, unit, terms,
    tok, yrecv, drecv, reduced, final, total,
    ld_sem, s1, r1, s0, r0, s2, r2, ws, wr, cs, cr, ys, yr, us, ur, fs, fr, ds, dr, es, er,
):
    pos, dpos = lax.axis_index("expert"), lax.axis_index("dp")
    z, x = pos // N, pos % N
    y, core = dpos // 2, dpos % 2
    expert = pos // (N * N // EXPERTS)

    def on_x(d):
        return {"expert": z * N + (x + d + N) % N}

    def on_z(d):
        return {"expert": ((z + d + N) % N) * N + x}

    def on_y(d):
        return {"dp": ((y + d + N) % N) * 2 + core}

    other = {"dp": y * 2 + (1 - core)}
    along = (on_z, on_x)
    here = (z, x)
    sent = []

    def remote(src, dst, ssem, rsem, dev):
        copy = pltpu.make_async_remote_copy(
            src_ref=src, dst_ref=dst, send_sem=ssem, recv_sem=rsem, device_id=dev, device_id_type=MESH
        )
        copy.start()
        sent.append(copy)
        return copy

    loads = [
        pltpu.make_async_copy(g_hbm, g_ref, ld_sem.at[0]),
        pltpu.make_async_copy(probs_hbm, probs_ref, ld_sem.at[1]),
        pltpu.make_async_copy(ids_hbm, ids_ref, ld_sem.at[2]),
        pltpu.make_async_copy(wdown_hbm, wdown, ld_sem.at[3]),
        pltpu.make_async_copy(gate_hbm, gate, ld_sem.at[4]),
        pltpu.make_async_copy(up_hbm, up, ld_sem.at[5]),
        pltpu.make_async_copy(wup_hbm, wup, ld_sem.at[6]),
        pltpu.make_async_copy(x_hbm.at[expert], xt, ld_sem.at[7]),
    ]
    for load in loads:
        load.start()

    barrier = pltpu.get_barrier_semaphore()
    partners = [on_x(d) for d in range(1, N)] + [on_z(d) for d in range(1, N)] + [on_y(d) for d in (1, -1, 2, -2)] + [other]
    for dev in partners:
        pl.semaphore_signal(barrier, inc=1, device_id=dev, device_id_type=MESH)

    for load in loads[0:3]:
        load.wait()
    lane32 = lax.broadcasted_iota(jnp.int32, (TOK, TOK), 1)
    row32 = lax.broadcasted_iota(jnp.int32, (TOK, TOK), 0)
    lane128 = lax.broadcasted_iota(jnp.int32, (TOK, 128), 1)
    shard[:, 384:512] = jnp.zeros((TOK, 128), BF16)
    shard[:, 0:448] = g_ref[...]
    tail = shard[:, 384:512].astype(F32)
    def column(row):
        return jnp.sum(jnp.where(lane32 == row32, row, 0.0), axis=1, keepdims=True)

    ids = ids_ref[...].astype(F32)
    expert_of_lane = ((lane128 - 64) // 4).astype(F32)
    ones = column(ids[0:1]) == expert_of_lane
    twos = column(ids[1:2]) == expert_of_lane
    prob = jnp.where(ones, column(probs_ref[0:1]), 0.0) + jnp.where(twos, column(probs_ref[1:2]), 0.0)
    used = jnp.where(ones, 1.0, 0.0) + jnp.where(twos, 1.0, 0.0)
    lower = jnp.where(lane32 < row32, 1.0, 0.0).astype(BF16)
    before = jnp.dot(lower, used.astype(BF16), preferred_element_type=F32)
    high = prob.astype(BF16).astype(F32)
    middle = (prob - high).astype(BF16).astype(F32)
    kind = lane128 % 4
    extra = jnp.where(kind == 0, high, jnp.where(kind == 1, middle, prob - high - middle))
    extra = jnp.where(kind == 3, used * (before + 1.0) - 1.0, extra)
    tail = jnp.where(lane128 >= 64, extra, tail)
    shard[:, 384:512] = tail.astype(BF16)
    for h in range(2):
        gath[h, here[h], 0] = shard[16 * h:16 * h + 16, :]

    pl.semaphore_wait(barrier, len(partners))

    first = {}
    for d in (1, 7, 2, 6, 3, 5, 4):
        for h in range(2):
            first[h, N - d] = remote(
                gath.at[h, here[h], 0], gath.at[h, here[h], N - d], s1.at[h, d - 1], r1.at[h, N - d - 1], along[1 - h](d)
            )
    loads[3].wait()
    down_swap = remote(wdown, wdown2, ws.at[0], wr.at[0], other)

    def piece(ref, h, index, c):
        return ref.at[h, index, pl.ds(2 * c, 2)]

    inflight = {}
    for j in (0, 1, 7, 2, 6, 3, 5, 4):
        for h in range(2):
            if j > 0:
                first[h, j].wait_recv()
            view = gath.at[h, here[h], j]
            for r in range(2):
                inflight[h, r, j] = remote(view, view, s0.at[j, h, r], r0.at[j, h, r], along[h](1 if r else -1))
    for k in (1, 2):
        for c in (0, 3, 1, 2):
            for h in range(2):
                for r in range(2):
                    sign, far = (1 if r else -1), hops(r, c)
                    if k == 1:
                        inflight[h, r, 2 * c].wait_recv()
                        inflight[h, r, 2 * c + 1].wait_recv()
                    else:
                        inflight[k - 1, c, h, r].wait_recv()
                    view = piece(gath, h, (here[h] - sign * k + N) % N, c)
                    if k == 2 and far == 4:
                        inflight[3, c, h, r] = remote(
                            view, view, s2.at[3, c, h, r], r2.at[3, c, h, r], along[h](2 * sign)
                        )
                    inflight[k, c, h, r] = remote(
                        view, view, s2.at[k, c, h, r], r2.at[k, c, h, r], along[h](sign)
                    )

    lane_id = lax.broadcasted_iota(jnp.int32, (128, ROWS), 1)
    step_id = lax.broadcasted_iota(jnp.int32, (128, 1), 0) // 16
    tail_lane = lax.broadcasted_iota(jnp.int32, (128, 128), 1) - 64 - 4 * expert

    def onehot_and_scaled(rows, source):
        extra = rows[:, 384:512].astype(F32)
        weight = jnp.sum(jnp.where((tail_lane >= 0) & (tail_lane < 3), extra, 0.0), axis=1, keepdims=True)
        rank = jnp.sum(jnp.where(tail_lane == 3, extra, 0.0), axis=1, keepdims=True)
        key = rank.astype(jnp.int32) * 16 + source
        return jnp.where(key == lane_id, 1.0, 0.0).astype(BF16), (rows.astype(F32) * weight).astype(BF16)

    def planes(offset, stride, count):
        def step(n, carry):
            zz = (z + offset + N + stride * n) % N
            xx = (x + offset + N + stride * n) % N
            low = pl.ds(pl.multiple_of((zz % 2) * 128, 128), 128)
            onehot, rows = onehot_and_scaled(
                gath[0, zz].reshape(128, 512), (zz % 2) * 8 + (x + step_id) % 8
            )
            place[zz // 2, low] = onehot
            scaled[zz // 2, low] = rows
            onehot, rows = onehot_and_scaled(
                gath[1, xx].reshape(128, 512), ((z + step_id) % 2) * 8 + xx
            )
            for j in range(N):
                zj = (z + j) % N
                at = pl.ds(pl.multiple_of(256 + (zj % 2) * 128 + xx * 16, 16), 16)
                place[zj // 2, at] = onehot[16 * j:16 * j + 16]
                scaled[zj // 2, at] = rows[16 * j:16 * j + 16]
            return carry

        lax.fori_loop(0, count, step, 0)

    planes(-2, 1, 5)
    for c in range(PIECES):
        for h in range(2):
            for r in range(2):
                inflight[2, c, h, r].wait_recv()
                if hops(r, c) == 4:
                    inflight[3, c, h, r].wait_recv()
    planes(3, 1, 3)

    def swap(g):
        span = pl.ds(pl.multiple_of(16 * g, 16), 16)
        return pltpu.make_async_remote_copy(
            src_ref=routed.at[pl.ds((1 - core) * 16, 16), span], dst_ref=routed2.at[:, span],
            send_sem=cs.at[g], recv_sem=cr.at[g], device_id=other, device_id_type=MESH,
        )

    def to_slots(g, carry):
        moved = lax.dot_general(place[g], scaled[g], (((0,), (0,)), ((), ())), preferred_element_type=F32)
        start = pl.multiple_of(16 * g, 16)
        routed[:, pl.ds(start, 16), :] = moved[:, 0:448].astype(BF16).reshape(CAP, 16, 448)
        swap(g).start()
        return carry

    lax.fori_loop(0, GROUPS, to_slots, 0)

    down_swap.wait_recv()
    for g in range(GROUPS):
        swap(g).wait_recv()

    def partial(offset, count):
        def step(n, carry):
            i = (y + offset + N + n) % N
            mine = routed[pl.ds(core * 16 + 2 * i, 2)].reshape(128, 448)
            theirs = routed2[pl.ds(2 * i, 2)].reshape(128, 448)
            dims = (((1,), (1,)), ((), ()))
            pair[i] = (
                lax.dot_general(wdown[...], mine, dims, preferred_element_type=F32)
                + lax.dot_general(wdown2[...], theirs, dims, preferred_element_type=F32)
            ).astype(BF16)
            return carry

        lax.fori_loop(0, count, step, 0)

    def down_blocks(low):
        def step(b, carry):
            span = pl.ds(pl.multiple_of(512 * b, 512), 512)
            hidden = (gate[:, span].astype(F32) * up[:, span].astype(F32)).astype(BF16)
            rows = routed[pl.ds(8 * b, 8)].reshape(512, 448)
            total[...] += jnp.dot(hidden, rows, preferred_element_type=F32)
            return carry

        lax.fori_loop(low, low + 2, step, 0)

    def ring_start(far, sign, view, recv, ssem, rsem, dev):
        copies = {}
        if far == 4:
            copies[0] = remote(view(4 * sign), recv(0), ssem(0), rsem(0), dev(2 * sign))
        copies[far - 3] = remote(view(3 * sign), recv(far - 3), ssem(far - 3), rsem(far - 3), dev(sign))
        return copies

    def ring_step(stage, copies, far, sign, view, recv, ssem, rsem, dev):
        own = view((3 - stage) * sign)
        value = own[...].astype(F32)
        for i in (0, 1) if (far, stage) == (4, 1) else (far + stage - 4,):
            copies[i].wait_recv()
            value = value + recv(i)[...].astype(F32)
        own[...] = value.astype(BF16)
        n = far + stage - 3
        copies[n] = remote(own, recv(n), ssem(n), rsem(n), dev(sign))

    def y_ring(c, r):
        low, size = SPLIT[c]
        return (
            hops(r, c),
            1 if r else -1,
            lambda offset: pair.at[(y + offset + N) % N, pl.ds(low, size)],
            lambda i: yrecv.at[i, c, r, pl.ds(0, size)],
            lambda i: ys.at[i, c, r],
            lambda i: yr.at[i, c, r],
            on_y,
        )

    inflight = {}
    partial(3, 3)
    for c in range(PIECES):
        for r in range(2):
            inflight[c, r] = ring_start(*y_ring(c, r))
    partial(-2, 5)
    total[...] = jnp.zeros_like(total)
    for load in loads[4:6]:
        load.wait()
    for stage in (1, 2):
        for c in range(PIECES):
            for r in range(2):
                ring_step(stage, inflight[c, r], *y_ring(c, r))
        down_blocks(2 * stage - 2)
    for load in loads[6:]:
        load.wait()

    mine = core * N + y
    lanes = pl.ds(pl.multiple_of(mine * 128, 128), 128)
    gathering = {}
    for c, (low, size) in enumerate(SPLIT):
        whole = pair[y, low:low + size].astype(F32)
        for r in range(2):
            inflight[c, r][hops(r, c) - 1].wait_recv()
            whole = whole + yrecv[hops(r, c) - 1, c, r, 0:size].astype(F32)
        unit[mine, low:low + size] = (whole * gate[low:low + size, lanes].astype(F32)).astype(BF16)
        view = unit.at[mine, pl.ds(low, size)]
        for r in range(2):
            gathering[0, c, r] = remote(view, view, us.at[0, c, r], ur.at[0, c, r], on_y(1 if r else -1))
    across = {}

    def cross_half(k, h, r, index):
        view = unit.at[core * N + index, pl.ds(HALVES[h][0], HALVES[h][1])]
        across[k, h, r] = remote(view, view, fs.at[k, h, r], fr.at[k, h, r], other)

    def slot_blocks(owner, offset, stride, count):
        def step(n, carry):
            b = owner * N + (y + offset + N + stride * n) % N
            rows = lax.dot_general(unit[b], wup[...], (((0,), (0,)), ((), ())), preferred_element_type=F32)
            terms[pl.ds(2 * b, 2)] = rows.astype(BF16).reshape(2, 64, 448)
            return carry

        lax.fori_loop(0, count, step, 0)

    def arrived(k):
        for h in range(2):
            for r in range(2):
                if (k, h, r) in across:
                    across[k, h, r].wait_recv()

    for h in range(2):
        cross_half(0, h, 1, y)
    gdown_out[...] = total[...].astype(BF16)
    slot_blocks(core, 0, 1, 1)
    for k in (1, 2, 3):
        if k == 3:
            arrived(2)
            slot_blocks(1 - core, -2, 4, 2)
        for c, (low, size) in enumerate(SPLIT):
            for r in range(2):
                sign, far = (1 if r else -1), hops(r, c)
                index = (y - sign * k + N) % N
                gathering[k - 1, c, r].wait_recv()
                view = unit.at[core * N + index, pl.ds(low, size)]
                if k == 2 and far == 4:
                    gathering[3, c, r] = remote(view, view, us.at[3, c, r], ur.at[3, c, r], on_y(2 * sign))
                if k < 3:
                    gathering[k, c, r] = remote(view, view, us.at[k, c, r], ur.at[k, c, r], on_y(sign))
                if c % 2 == 1:
                    cross_half(k, c // 2, r, index)
        if k < 3:
            slot_blocks(core, -k, 2 * k, 2)
            arrived(k - 1)
            slot_blocks(1 - core, 1 - k, 2 * k - 2, min(k, 2))
    for c in range(PIECES):
        for r in range(2):
            if hops(r, c) == 4:
                gathering[3, c, r].wait_recv()
                if c % 2 == 1:
                    cross_half(4, c // 2, r, (y + 4) % N)
    slot_blocks(core, 3, 1, 3)
    arrived(3)
    arrived(4)
    slot_blocks(1 - core, 3, 1, 3)
    total[...] = jnp.zeros_like(total)

    def to_tokens(n, carry):
        g = (z // 2 + 1 + n) % GROUPS
        start = pl.multiple_of(16 * g, 16)
        rows = terms[:, pl.ds(start, 16), :].reshape(ROWS, 448)
        back = jnp.dot(place[g], rows, preferred_element_type=F32).astype(BF16)
        tok[0, pl.ds(2 * g, 2)] = back[0:256].reshape(2, N, 16, 448)
        tok[1, :, (2 * g - z + N) % N] = back[256:384].reshape(N, 16, 448)
        tok[1, :, (2 * g + 1 - z + N) % N] = back[384:512].reshape(N, 16, 448)
        return carry

    def token_ring(c, h, r):
        return (
            hops(r, c),
            1 if r else -1,
            lambda offset: piece(tok, h, (here[h] + offset + N) % N, c),
            lambda i: drecv.at[i, c, h, r],
            lambda i: ds.at[i, c, h, r],
            lambda i: dr.at[i, c, h, r],
            along[h],
        )

    def up_blocks(low, count):
        def step(b, carry):
            span = pl.ds(pl.multiple_of(b * 128, 128), 128)
            total[...] += lax.dot_general(
                unit[b], xt[:, span], (((1,), (1,)), ((), ())), preferred_element_type=F32
            )
            return carry

        lax.fori_loop(low, low + count, step, 0)

    inflight = {}
    lax.fori_loop(0, GROUPS - 1, to_tokens, 0)
    for stage in range(3):
        if stage == 0:
            for h in range(2):
                for c in range(PIECES):
                    for r in range(2):
                        inflight[c, h, r] = ring_start(*token_ring(c, h, r))
                if h == 0:
                    lax.fori_loop(GROUPS - 1, GROUPS, to_tokens, 0)
        else:
            for c in range(PIECES):
                for h in range(2):
                    for r in range(2):
                        ring_step(stage, inflight[c, h, r], *token_ring(c, h, r))
        up_blocks((0, 6, 11)[stage], (6, 5, 5)[stage])
    gup_out[...] = total[...].astype(BF16)

    last = []
    for c in range(PIECES):
        for h in range(2):
            whole = piece(tok, h, here[h], c)[...].astype(F32)
            for r in range(2):
                inflight[c, h, r][hops(r, c) - 1].wait_recv()
                whole = whole + drecv[hops(r, c) - 1, c, h, r].astype(F32)
            reduced[h, 2 * c:2 * c + 2] = whole.astype(BF16)
            for d in (2 * c, 2 * c + 1):
                if d > 0:
                    last.append(
                        remote(reduced.at[h, d], final.at[h, d - 1], es.at[h, d - 1], er.at[h, d - 1], along[1 - h](d))
                    )
    for copy in last:
        copy.wait_recv()
    for h in range(2):
        whole = reduced[h, 0].astype(F32)
        for d in range(1, N):
            whole = whole + final[h, d - 1].astype(F32)
        tok_out[16 * h:16 * h + 16, :] = whole.astype(BF16)
    for copy in sent:
        copy.wait_send()
    for g in range(GROUPS):
        swap(g).wait_send()


def body(grad_out, probs, expert_ids, x_saved, gate_act, up_act, w_up, w_down):
    vmem, hbm = pl.BlockSpec(memory_space=pltpu.VMEM), pl.BlockSpec(memory_space=pl.ANY)
    dma = pltpu.SemaphoreType.DMA
    units, width, slots = 304, 448, 2048
    outs = pl.pallas_call(
        kernel,
        out_shape=(
            jax.ShapeDtypeStruct((TOK, width), BF16),
            jax.ShapeDtypeStruct((units, width), BF16),
            jax.ShapeDtypeStruct((units, width), BF16),
        ),
        in_specs=[hbm] * 8,
        out_specs=(vmem, vmem, vmem),
        scratch_shapes=[
            pltpu.VMEM((TOK, width), BF16),
            pltpu.VMEM((2, TOK), F32),
            pltpu.VMEM((2, TOK), jnp.int32),
            pltpu.VMEM((TOK, 512), BF16),
            pltpu.VMEM((2, N, N, 16, 512), BF16),
            pltpu.VMEM((GROUPS, ROWS, ROWS), BF16),
            pltpu.VMEM((GROUPS, ROWS, 512), BF16),
            pltpu.VMEM((CAP, N * N, width), BF16),
            pltpu.VMEM((CAP // 2, N * N, width), BF16),
            pltpu.VMEM((units, width), BF16),
            pltpu.VMEM((units, width), BF16),
            pltpu.VMEM((units, width), BF16),
            pltpu.VMEM((units, slots), BF16),
            pltpu.VMEM((units, slots), BF16),
            pltpu.VMEM((width, slots), BF16),
            pltpu.VMEM((N, units, 128), BF16),
            pltpu.VMEM((2 * N, units, 128), BF16),
            pltpu.VMEM((CAP, N * N, width), BF16),
            pltpu.VMEM((2, N, N, 16, width), BF16),
            pltpu.VMEM((4, PIECES, 2, 80, 128), BF16),
            pltpu.VMEM((4, PIECES, 2, 2, 2, 16, width), BF16),
            pltpu.VMEM((2, N, 16, width), BF16),
            pltpu.VMEM((2, N - 1, 16, width), BF16),
            pltpu.VMEM((units, width), F32),
            dma((8,)),
            dma((2, N - 1)), dma((2, N - 1)),
            dma((N, 2, 2)), dma((N, 2, 2)),
            dma((4, PIECES, 2, 2)), dma((4, PIECES, 2, 2)),
            dma((1,)), dma((1,)),
            dma((GROUPS,)), dma((GROUPS,)),
            dma((4, PIECES, 2)), dma((4, PIECES, 2)),
            dma((4, PIECES, 2)), dma((4, PIECES, 2)),
            dma((5, 2, 2)), dma((5, 2, 2)),
            dma((4, PIECES, 2, 2)), dma((4, PIECES, 2, 2)),
            dma((2, N - 1)), dma((2, N - 1)),
        ],
        compiler_params=pltpu.CompilerParams(
            collective_id=0, has_side_effects=True, vmem_limit_bytes=60 * 1024 * 1024
        ),
        cost_estimate=pl.CostEstimate(flops=4_000_000_000, bytes_accessed=8_000_000, transcendentals=0),
    )(
        grad_out,
        probs.T,
        expert_ids.T,
        jnp.swapaxes(x_saved, 1, 2),
        gate_act.T,
        up_act.T,
        w_up.T,
        w_down,
    )
    return outs[0], outs[1].T, outs[2]


def solution(mesh):
    return jax.shard_map(
        body,
        mesh=mesh,
        in_specs=(
            P("expert", "dp"),
            P("expert", None),
            P("expert", None),
            P(None, None, "dp"),
            P(None, "expert"),
            P(None, "expert"),
            P("dp", "expert"),
            P("expert", "dp"),
        ),
        out_specs=(P("expert", "dp"), P("dp", "expert"), P("expert", "dp")),
        check_vma=False,
    )
```
